32 devices in a mesh: seq: 8 (over z, y), dp: 4 (over x, core).
Axes of the slice: x: 2, y: 2, z: 4, core: 2. Of those that a mesh axis runs over, the one named last changes fastest.
Arguments:
- resid: bfloat16 [4, 4096, 2048], P('dp', 'seq'), may hold values from -6 to 6
- token_ids: int32 [4, 4096], P('dp', 'seq'), may hold values from 0 to 63999
- code_proj: float32 [6, 2048], replicated, may hold values from -2.5 to 2.5
- w_query: bfloat16 [2048, 1024], replicated, may hold values from -0.125 to 0.125
- w_key: bfloat16 [2048, 1024], replicated, may hold values from -0.125 to 0.125
- w_value: bfloat16 [2048, 1024], replicated, may hold values from -0.125 to 0.125
- gain: float32 [1024], replicated, may hold values from 0.1 to 1.9
- out_grad: bfloat16 [4, 4096, 1024], P('dp', 'seq'), may hold values from -6 to 6
Outputs:
- resid_grad: bfloat16 [4, 4096, 2048], P('dp', 'seq')
- weight_grads: float32 [2048, 3, 1024], P(('seq', 'dp'))
- gain_grad: float32 [1024], replicated
- code_grad: float32 [6, 2048], replicated
The draws below stay inside these ranges and needn't reach their ends.
Inputs may be any that keep to these rules, and one draw needn't show every extreme that they name: `token_ids`: ids of the codebook of 64000 codes.
All inputs are finite; a program needn't handle non-finite values.
Results may differ from the reference program's by a relative error of at most 0.0084.
Values sent between devices are 32-bit elements; how exact they have to be, the bound alone decides.
No kernel may reach another device: no remote copies, remote signals or barrier semaphores. Data moves between devices by JAX's collectives and lax.ppermute only.
A program may use at most 128 MiB of HBM per device.

```python
import math
import jax
import jax.numpy as jnp
import numpy as np
from jax import lax

D = 2048
HEADS = 8
DH = 128
HD = 1024
CODES = 6
VOCAB = 64000
TOK_DEV = 512
SEQ_LEN = 4096
BATCH = 4
N_SEQ = 8


def plant(values, key, smallest, high):
    place = [jax.random.randint(jax.random.fold_in(key, axis), (), 0, length) for axis, length in enumerate(values.shape)]
    main_axis = values.shape.index(max(values.shape))
    next_to = place[:main_axis] + [(place[main_axis] + 1) % values.shape[main_axis]] + place[main_axis + 1:]
    return values.at[tuple(place)].set(smallest).at[tuple(next_to)].set(high)


def level_of(stream_key, dims, split, least, top_value):
    def one(axis_at, parts):
        draws = jax.random.uniform(jax.random.fold_in(jax.random.fold_in(stream_key, 6), axis_at), (parts,), jnp.float32, least / len(split), top_value / len(split))
        return jnp.repeat(jnp.exp(draws), dims[axis_at] // parts).reshape((-1,) + (1,) * (len(dims) - axis_at - 1))

    factor_of = one(*split[0])
    for cut in split[1:]:
        factor_of = factor_of * one(*cut)
    return factor_of


def rank_table(amount, skew):
    loads = [(1 << 20) // math.isqrt(grade ** skew) + 1 for grade in range(1, amount + 1)]
    deviation = 1 + sum(loads) // (1 << 30)
    return np.cumsum(np.array([max(1, weight // deviation) for weight in loads]))


def ranked(own_key, shape, count, slope):
    grid = rank_table(count, slope)
    ticket = jax.random.randint(jax.random.fold_in(own_key, 1), shape, 0, int(grid[count - 1]))
    grade = jnp.searchsorted(jnp.asarray(grid, jnp.int32), ticket, side="right")
    return jax.random.permutation(jax.random.fold_in(own_key, 2), count)[grade].astype(jnp.int32)


def centred(rng, dims, scale, limit, shards=(), dtype=jnp.bfloat16):
    entries = scale * jax.random.normal(rng, dims, jnp.float32)
    if shards:
        entries = entries * level_of(rng, dims, shards, -0.22, 0.18)
    return jnp.clip(entries, -limit, limit).astype(dtype)


def setup_inputs(seed: int = 0) -> dict:
    streams_of = jax.random.split(jax.random.key(seed), 9)
    return {
        "resid": centred(streams_of[0], (BATCH, SEQ_LEN, D), 1.0, 6.0, ((0, 4), (1, 8))),
        "token_ids": plant(ranked(streams_of[1], (BATCH, SEQ_LEN), VOCAB, 2), jax.random.fold_in(streams_of[1], 3), 0, VOCAB - 1).astype(jnp.int32),
        "code_proj": centred(streams_of[2], (CODES, D), CODES ** -0.5, 2.5, (), jnp.float32),
        "w_query": centred(streams_of[3], (D, HD), D ** -0.5, 0.125),
        "w_key": centred(streams_of[4], (D, HD), D ** -0.5, 0.125),
        "w_value": centred(streams_of[5], (D, HD), D ** -0.5, 0.125),
        "gain": jnp.clip(1.0 + 0.18 * jax.random.normal(streams_of[6], (HD,), jnp.float32), 0.1, 1.9),
        "out_grad": centred(streams_of[7], (BATCH, SEQ_LEN, HD), 1.0, 6.0, ((0, 4), (1, 8))),
    }


fsq_levels = (8, 8, 8, 5, 5, 5)
fsq_bases = (1, 8, 64, 512, 2560, 12800)

def code_rows(token_ids):
    code_list = []
    for fsq_level, fsq_base in zip(fsq_levels, fsq_bases):
        fsq_digit = token_ids // fsq_base % fsq_level
        code_list.append((2.0 * fsq_digit.astype(jnp.float32) - (fsq_level - 1)) / (fsq_level - 1))
    return jnp.stack(code_list)

def silu_slope(value):
    sigma = jax.nn.sigmoid(value)
    return sigma * (1.0 + value * (1.0 - sigma))

def reference(resid, token_ids, code_proj, w_query, w_key, w_value, gain, out_grad):
    f32 = jnp.float32
    codes = code_rows(token_ids)
    summed = resid.astype(f32)
    for index in range(codes.shape[0]):
        summed = summed + codes[index][..., None] * code_proj[index]
    inputs = summed.astype(jnp.bfloat16).reshape(BATCH * SEQ_LEN, D)
    query_pre = jnp.dot(inputs, w_query, preferred_element_type=f32)
    key_pre = jnp.dot(inputs, w_key, preferred_element_type=f32)
    value_pre = jnp.dot(inputs, w_value, preferred_element_type=f32)

    def to_heads(array):
        return array.reshape(BATCH, N_SEQ, TOK_DEV, HEADS, DH).transpose(1, 0, 3, 2, 4)

    def from_heads(array):
        return array.transpose(1, 0, 3, 2, 4).reshape(BATCH * SEQ_LEN, HD)
    queries = to_heads(jax.nn.silu(query_pre).astype(jnp.bfloat16))
    keys = to_heads(jax.nn.silu(key_pre).astype(jnp.bfloat16))
    values = to_heads(value_pre.astype(jnp.bfloat16))
    grads_out = to_heads(out_grad)
    gain_heads = gain.reshape(HEADS, 1, DH)
    block_kv = jnp.einsum('cbhte,cbhtd->cbhed', keys.astype(f32), values.astype(f32))
    empty_state = jnp.zeros_like(block_kv[:1])
    prefix = jnp.concatenate([empty_state, jnp.cumsum(block_kv, axis=0)[:-1]], axis=0).astype(jnp.bfloat16)
    row_ids = lax.broadcasted_iota(jnp.int32, (TOK_DEV, TOK_DEV), 0)
    col_ids = lax.broadcasted_iota(jnp.int32, (TOK_DEV, TOK_DEV), 1)
    causal = col_ids <= row_ids

    def block_scores(query_blk, key_blk):
        raw = jnp.einsum('bhte,bhse->bhts', query_blk.astype(f32), key_blk.astype(f32))
        return jnp.where(causal, raw, 0.0).astype(jnp.bfloat16)

    def forward_block(operands):
        query_blk, key_blk, value_blk, prefix_blk, grad_blk = operands
        scores = block_scores(query_blk, key_blk)
        attended = jnp.einsum('bhts,bhsd->bhtd', scores.astype(f32), value_blk.astype(f32))
        attended = attended + jnp.einsum('bhte,bhed->bhtd', query_blk.astype(f32), prefix_blk.astype(f32))
        root = jnp.sqrt(lax.optimization_barrier(jnp.mean(attended * attended, axis=-1, keepdims=True)) + 1e-06)
        normed = attended / root
        d_normed = grad_blk.astype(f32) * gain_heads
        d_att = ((d_normed - normed * lax.optimization_barrier(jnp.mean(d_normed * normed, axis=-1, keepdims=True))) / root).astype(jnp.bfloat16)
        gain_term = lax.optimization_barrier(jnp.sum(grad_blk.astype(f32) * normed, axis=2))
        return (d_att, gain_term)
    d_att, gain_terms = lax.map(forward_block, (queries, keys, values, prefix, grads_out))
    block_grad = jnp.einsum('cbhte,cbhtd->cbhed', queries.astype(f32), d_att.astype(f32))
    inclusive = jnp.flip(jnp.cumsum(jnp.flip(block_grad, axis=0), axis=0), axis=0)
    suffix = jnp.concatenate([inclusive[1:], empty_state], axis=0).astype(jnp.bfloat16)

    def backward_block(operands):
        query_blk, key_blk, value_blk, prefix_blk, suffix_blk, datt_blk = operands
        q32 = query_blk.astype(f32)
        k32 = key_blk.astype(f32)
        v32 = value_blk.astype(f32)
        a32 = datt_blk.astype(f32)
        p32 = prefix_blk.astype(f32)
        s32 = suffix_blk.astype(f32)
        scores = block_scores(query_blk, key_blk).astype(f32)
        back_scores = jnp.where(causal, jnp.einsum('bhtd,bhsd->bhts', a32, v32), 0.0).astype(jnp.bfloat16).astype(f32)
        d_query = jnp.einsum('bhts,bhse->bhte', back_scores, k32) + jnp.einsum('bhtd,bhed->bhte', a32, p32)
        d_key = jnp.einsum('bhts,bhte->bhse', back_scores, q32) + jnp.einsum('bhsd,bhed->bhse', v32, s32)
        d_value = jnp.einsum('bhts,bhtd->bhsd', scores, a32) + jnp.einsum('bhse,bhed->bhsd', k32, s32)
        return (d_query, d_key, d_value)
    d_query, d_key, d_value = lax.map(backward_block, (queries, keys, values, prefix, suffix, d_att))
    grad_q = (from_heads(d_query) * silu_slope(query_pre)).astype(jnp.bfloat16)
    grad_k = (from_heads(d_key) * silu_slope(key_pre)).astype(jnp.bfloat16)
    grad_v = from_heads(d_value).astype(jnp.bfloat16)
    transpose_dims = (((1,), (1,)), ((), ()))
    input_grad = lax.dot_general(grad_q, w_query, transpose_dims, preferred_element_type=f32)
    input_grad = input_grad + lax.dot_general(grad_k, w_key, transpose_dims, preferred_element_type=f32)
    input_grad = input_grad + lax.dot_general(grad_v, w_value, transpose_dims, preferred_element_type=f32)
    resid_grad = input_grad.astype(jnp.bfloat16).reshape(BATCH, SEQ_LEN, D)
    grad_scale = 1.0 / math.sqrt(BATCH * SEQ_LEN)
    row_dims = (((0,), (0,)), ((), ()))
    weight_grads = jnp.stack([lax.dot_general(inputs, grad_part, row_dims, preferred_element_type=f32) for grad_part in (grad_q, grad_k, grad_v)], axis=1) * grad_scale
    gain_grad = lax.optimization_barrier(jnp.sum(gain_terms, axis=(0, 1))).reshape(HD) * grad_scale
    code_grad = jnp.dot(codes.reshape(codes.shape[0], BATCH * SEQ_LEN), input_grad, precision=lax.Precision.HIGHEST) * grad_scale
    return (resid_grad, weight_grads, gain_grad, code_grad)
```

```python
import functools
import math

import jax
import jax.numpy as jnp
from jax import lax
from jax.experimental import pallas as pl
from jax.experimental.pallas import tpu as pltpu
from jax.sharding import PartitionSpec as P

HEADS = 8
DH = 128
PAIR = 2
WIDE = PAIR * DH
AXES = ("seq", "dp")
F32 = jnp.float32
BF16 = jnp.bfloat16

fsq_levels = (8, 8, 8, 5, 5, 5)
fsq_bases = (1, 8, 64, 512, 2560, 12800)

NT = (((1,), (1,)), ((), ()))
TN = (((0,), (0,)), ((), ()))


def mm(a, b):
    return jnp.dot(a, b, preferred_element_type=F32)


def mm_nt(a, b):
    return lax.dot_general(a, b, NT, preferred_element_type=F32)


def mm_tn(a, b):
    return lax.dot_general(a, b, TN, preferred_element_type=F32)


def params():
    return pltpu.CompilerParams(vmem_limit_bytes=48 * 1024 * 1024)


def cost(flops, moved):
    return pl.CostEstimate(flops=int(flops), bytes_accessed=int(moved), transcendentals=0)


def shape(dims, dtype):
    return jax.ShapeDtypeStruct(dims, dtype)


def code_rows(token_ids):
    code_list = []
    for fsq_level, fsq_base in zip(fsq_levels, fsq_bases):
        fsq_digit = token_ids // fsq_base % fsq_level
        code_list.append((2.0 * fsq_digit.astype(F32) - (fsq_level - 1)) / (fsq_level - 1))
    return jnp.stack(code_list)


def silu_and_slope(value):
    sigma = 1.0 / (1.0 + jnp.exp(-value))
    return value * sigma, sigma * (1.0 + value * (1.0 - sigma))


def columns(rows):
    return pl.BlockSpec((rows, WIDE), lambda p, *_: (0, p))


def states():
    return pl.BlockSpec((PAIR, DH, DH), lambda p, *_: (p, 0, 0))


def picked_states():
    return pl.BlockSpec((1, PAIR, DH, DH), lambda p, owner: (owner[0] ^ p, 0, 0, 0))


def whole(dims):
    return pl.BlockSpec(dims, lambda p, *_: (0,) * len(dims))


def kv_kernel(x_ref, wk_ref, wv_ref, k_ref, slope_ref, v_ref, kv_ref):
    x = x_ref[...]
    key, slope = silu_and_slope(mm(x, wk_ref[...]))
    key = key.astype(BF16)
    value = mm(x, wv_ref[...]).astype(BF16)
    k_ref[...] = key
    slope_ref[...] = slope
    v_ref[...] = value
    for h in range(PAIR):
        at = slice(h * DH, (h + 1) * DH)
        kv_ref[h] = mm_tn(key[:, at], value[:, at])


def keys_values(x, w_key, w_value):
    t, d = x.shape
    hd = w_key.shape[1]
    return pl.pallas_call(
        kv_kernel,
        grid=(hd // WIDE,),
        in_specs=[whole((t, d)), columns(d), columns(d)],
        out_specs=[columns(t), columns(t), columns(t), states()],
        out_shape=[
            shape((t, hd), BF16),
            shape((t, hd), F32),
            shape((t, hd), BF16),
            shape((hd // DH, DH, DH), F32),
        ],
        compiler_params=params(),
        cost_estimate=cost(4 * t * d * hd, 4 * d * hd + 10 * t * hd),
        name="keys_values",
    )(x, w_key, w_value)


def causal_mask(t, transposed):
    rows = lax.broadcasted_iota(jnp.int32, (t, t), 0)
    cols = lax.broadcasted_iota(jnp.int32, (t, t), 1)
    return rows <= cols if transposed else cols <= rows


def query_kernel(x_ref, wq_ref, k_ref, v_ref, q_ref, slope_ref, sv_ref):
    t = x_ref.shape[0]
    query, slope = silu_and_slope(mm(x_ref[...], wq_ref[...]))
    query = query.astype(BF16)
    q_ref[...] = query
    slope_ref[...] = slope
    mask = causal_mask(t, False)
    for h in range(PAIR):
        at = slice(h * DH, (h + 1) * DH)
        scores = jnp.where(mask, mm_nt(query[:, at], k_ref[:, at]), 0.0).astype(BF16)
        sv_ref[:, at] = mm(scores, v_ref[:, at])


def queries_scores(x, w_query, keys, values):
    t, d = x.shape
    hd = w_query.shape[1]
    return pl.pallas_call(
        query_kernel,
        grid=(hd // WIDE,),
        in_specs=[whole((t, d)), columns(d), columns(t), columns(t)],
        out_specs=[columns(t), columns(t), columns(t)],
        out_shape=[shape((t, hd), BF16), shape((t, hd), F32), shape((t, hd), F32)],
        compiler_params=params(),
        cost_estimate=cost(2 * t * d * hd + 4 * t * t * hd, 2 * d * hd + 14 * t * hd),
        name="queries_scores",
    )(x, w_query, keys, values)


def norm_kernel(owner, sv_ref, q_ref, prefix_ref, og_ref, gain_ref, datt_ref, term_ref, grad_ref):
    for h in range(PAIR):
        at = slice(h * DH, (h + 1) * DH)
        query = q_ref[:, at]
        attended = sv_ref[:, at] + mm(query, prefix_ref[0, h].astype(BF16))
        inverse = lax.rsqrt(jnp.mean(attended * attended, axis=-1, keepdims=True) + 1e-06)
        normed = attended * inverse
        grad = og_ref[:, at].astype(F32)
        term_ref[:, at] = jnp.sum(grad * normed, axis=0, keepdims=True)
        d_normed = grad * gain_ref[:, at]
        inner = jnp.mean(d_normed * normed, axis=-1, keepdims=True)
        d_att = ((d_normed - normed * inner) * inverse).astype(BF16)
        datt_ref[:, at] = d_att
        grad_ref[h] = mm_tn(query, d_att)


def norm_gradient(owner, sv, queries, prefix, out_grad, gain):
    t, hd = sv.shape
    return pl.pallas_call(
        norm_kernel,
        grid_spec=pltpu.PrefetchScalarGridSpec(
            num_scalar_prefetch=1,
            grid=(hd // WIDE,),
            in_specs=[columns(t), columns(t), picked_states(), columns(t), columns(1)],
            out_specs=[columns(t), columns(1), states()],
        ),
        out_shape=[shape((t, hd), BF16), shape((1, hd), F32), shape((hd // DH, DH, DH), F32)],
        compiler_params=params(),
        cost_estimate=cost(4 * t * hd * DH, 10 * t * hd),
        name="norm_gradient",
    )(owner, sv, queries, prefix, out_grad, gain)


def dquery_kernel(owner, datt_ref, v_ref, k_ref, prefix_ref, slope_ref, g16_ref, g32_ref):
    t = datt_ref.shape[0]
    mask = causal_mask(t, False)
    for h in range(PAIR):
        at = slice(h * DH, (h + 1) * DH)
        d_att = datt_ref[:, at]
        back = jnp.where(mask, mm_nt(d_att, v_ref[:, at]), 0.0).astype(BF16)
        d_query = mm(back, k_ref[:, at]) + mm_nt(d_att, prefix_ref[0, h].astype(BF16))
        grad = (d_query * slope_ref[:, at]).astype(BF16)
        g16_ref[:, at] = grad
        g32_ref[:, at] = grad.astype(F32)


def query_gradient(owner, d_att, values, keys, prefix, slope):
    t, hd = d_att.shape
    return pl.pallas_call(
        dquery_kernel,
        grid_spec=pltpu.PrefetchScalarGridSpec(
            num_scalar_prefetch=1,
            grid=(hd // WIDE,),
            in_specs=[columns(t), columns(t), columns(t), picked_states(), columns(t)],
            out_specs=[columns(t), columns(t)],
        ),
        out_shape=[shape((t, hd), BF16), shape((t, hd), F32)],
        compiler_params=params(),
        cost_estimate=cost(4 * t * t * hd, 16 * t * hd),
        name="query_gradient",
    )(owner, d_att, values, keys, prefix, slope)


def within_kernel(datt_ref, v_ref, k_ref, q_ref, dk_ref, dv_ref):
    t = datt_ref.shape[0]
    mask = causal_mask(t, True)
    for h in range(PAIR):
        at = slice(h * DH, (h + 1) * DH)
        d_att, query = datt_ref[:, at], q_ref[:, at]
        back = jnp.where(mask, mm_nt(v_ref[:, at], d_att), 0.0).astype(BF16)
        dk_ref[:, at] = mm(back, query)
        scores = jnp.where(mask, mm_nt(k_ref[:, at], query), 0.0).astype(BF16)
        dv_ref[:, at] = mm(scores, d_att)


def within_block(d_att, values, keys, queries):
    t, hd = d_att.shape
    return pl.pallas_call(
        within_kernel,
        grid=(hd // WIDE,),
        in_specs=[columns(t)] * 4,
        out_specs=[columns(t), columns(t)],
        out_shape=[shape((t, hd), F32), shape((t, hd), F32)],
        compiler_params=params(),
        cost_estimate=cost(8 * t * t * hd, 16 * t * hd),
        name="within_block",
    )(d_att, values, keys, queries)


def dkv_kernel(owner, dk_ref, dv_ref, v_ref, k_ref, suffix_ref, slope_ref, k16, k32, v16, v32):
    for h in range(PAIR):
        at = slice(h * DH, (h + 1) * DH)
        suffix = suffix_ref[0, h].astype(BF16)
        grad = ((dk_ref[:, at] + mm_nt(v_ref[:, at], suffix)) * slope_ref[:, at]).astype(BF16)
        k16[:, at] = grad
        k32[:, at] = grad.astype(F32)
        grad = (dv_ref[:, at] + mm(k_ref[:, at], suffix)).astype(BF16)
        v16[:, at] = grad
        v32[:, at] = grad.astype(F32)


def key_value_gradients(owner, dk, dv, values, keys, suffix, slope):
    t, hd = dk.shape
    return pl.pallas_call(
        dkv_kernel,
        grid_spec=pltpu.PrefetchScalarGridSpec(
            num_scalar_prefetch=1,
            grid=(hd // WIDE,),
            in_specs=[columns(t)] * 4 + [picked_states(), columns(t)],
            out_specs=[columns(t)] * 4,
        ),
        out_shape=[shape((t, hd), BF16), shape((t, hd), F32)] * 2,
        compiler_params=params(),
        cost_estimate=cost(4 * t * hd * DH, 28 * t * hd),
        name="key_value_gradients",
    )(owner, dk, dv, values, keys, suffix, slope)


def exchange(array, axis, mask):
    count = lax.axis_size(axis)
    return lax.ppermute(array, axis, [(i, i ^ mask) for i in range(count)])


def entering(part, reverse):
    count = lax.axis_size("seq")
    group = min(HEADS // PAIR, count)
    clusters = count // group
    place = lax.axis_index("seq")
    if reverse:
        place = count - 1 - place
    inner, cluster = place % group, place // group
    twist = group // 2
    owner = inner ^ (twist * (cluster % 2))
    pieces = part.reshape(group, HEADS // group, DH, DH)

    def piece(index):
        return lax.dynamic_index_in_dim(pieces, index, 0, False)

    blocks = [piece(owner)]
    for mask in range(1, group):
        blocks.append(exchange(piece(owner ^ mask), "seq", mask))
    total = sum(blocks[1:], blocks[0])
    base = jnp.zeros_like(total)
    for shift in range(1, clusters):
        pairs = []
        for source in range(clusters - shift):
            for slot in range(group):
                a = source * group + (slot ^ (twist * (source % 2)))
                target = source + shift
                b = target * group + (slot ^ (twist * (target % 2)))
                pairs.append((count - 1 - a, count - 1 - b) if reverse else (a, b))
        base = base + lax.ppermute(total, "seq", pairs)
    outs = []
    for mask in range(group):
        local = base
        for other in range(group):
            if other != mask:
                local = local + jnp.where((inner ^ other) < (inner ^ mask), blocks[other], 0.0)
        outs.append(exchange(local, "seq", mask) if mask else local)
    return jnp.stack(outs), owner.astype(jnp.int32).reshape(1)


def sum_everywhere(array):
    for axis in AXES:
        step = 1
        while step < lax.axis_size(axis):
            array = array + exchange(array, axis, step)
            step *= 2
    return array


def merge_kernel(own_ref, other_ref, out_ref):
    half = own_ref.shape[1]
    out_ref[:, :half] = own_ref[...]
    out_ref[:, half:] = other_ref[...].astype(BF16)


def merge(own, other):
    rows, t = own.shape
    return pl.pallas_call(
        merge_kernel,
        out_shape=shape((rows, 2 * t), BF16),
        compiler_params=params(),
        cost_estimate=cost(0, 10 * rows * t),
        name="merge",
    )(own, other)


def product_kernel(picks, cuts, x_ref, own_ref, other_ref, *out_refs):
    grads = jnp.concatenate([own_ref[...], other_ref[...].astype(BF16)], axis=0)
    depth = grads.shape[0]
    for out_ref, pick, (start, stop) in zip(out_refs, picks, cuts):
        rows = x_ref[pick].reshape(-1, depth)
        out_ref[...] = mm(rows, grads[:, start:stop]).reshape(out_ref.shape)


def products(x, own, other, picks, cuts):
    dims = x.shape
    kept = math.prod(dims[:-1]) // 2
    return pl.pallas_call(
        functools.partial(product_kernel, picks, cuts),
        out_shape=[
            shape((2,) * (len(dims) - 3) + (dims[-2], stop - start), F32) for start, stop in cuts
        ],
        compiler_params=params(),
        cost_estimate=cost(2 * kept * dims[-1] * own.shape[1], 2 * x.size + 6 * own.size + 4 * kept * own.shape[1]),
        name="weight_products",
    )(x, own, other)


def at_axis(count, axis, index):
    return (slice(None),) * axis + (index,) + (slice(None),) * (count - axis - 1)


def scattered(x, own, other, masks, orders, cuts):
    count = len(masks)
    sent = products(x, own, other, [at_axis(count, order[0], 1) for order in orders], cuts)
    kept = products(x, own, other, [at_axis(count, order[0], 0) for order in orders], cuts)
    outs = []
    for order, first, rest in zip(orders, sent, kept):
        left = list(range(count))
        sending = first
        for at, axis in enumerate(order):
            got = both_exchange(sending, masks[axis])
            left.remove(axis)
            if at + 1 < len(order):
                place = left.index(order[at + 1])
                sending = rest[at_axis(len(left), place, 1)] + got[at_axis(len(left), place, 1)]
                rest = rest[at_axis(len(left), place, 0)] + got[at_axis(len(left), place, 0)]
            else:
                rest = rest + got
        outs.append(rest)
    return jnp.concatenate(outs, axis=-1)


def both_exchange(array, mask):
    total = lax.axis_size("seq") * lax.axis_size("dp")
    return lax.ppermute(array, AXES, [(i, i ^ mask) for i in range(total)])


def body(resid, token_ids, code_proj, w_query, w_key, w_value, gain, out_grad):
    positions, width = resid.shape[1:]
    features = w_query.shape[1]
    n_seq, n_dp = lax.axis_size("seq"), lax.axis_size("dp")
    total = n_seq * n_dp
    me = lax.axis_index("seq") * n_dp + lax.axis_index("dp")
    code_values = code_rows(token_ids[0])
    summed = resid[0].astype(F32)
    for index in range(code_values.shape[0]):
        summed = summed + code_values[index][:, None] * code_proj[index]
    inputs = summed.astype(BF16)

    keys, key_slope, values, block_kv = keys_values(inputs, w_key, w_value)
    prefix, owner = entering(block_kv, False)
    queries, query_slope, within = queries_scores(inputs, w_query, keys, values)

    bits = total.bit_length() - 1
    masks = [1 << b for b in range(1, bits)]
    masks[-1] |= masks[-2]
    rows = width // total
    turned = inputs.T.reshape(total // 2, 2, rows, positions)
    core, chip = me % 2, me // 2
    offsets = []
    for pick in range(1 << (bits - 1)):
        offset = 0
        for place, mask in enumerate(masks):
            if pick >> (bits - 2 - place) & 1:
                offset ^= mask >> 1
        offsets.append(offset)

    def ordered(which):
        mine = lax.dynamic_index_in_dim(turned, which, 1, False)
        return jnp.concatenate(
            [lax.dynamic_index_in_dim(mine, chip ^ offset, 0, False) for offset in offsets], axis=0
        )

    own_rows = ordered(core)
    other_rows = both_exchange(ordered(1 - core).astype(F32), 1)
    x = merge(own_rows, other_rows).reshape((2,) * (bits - 1) + (rows, 2 * positions))

    gain_row = gain.reshape(1, features)
    d_att, gain_term, block_grad = norm_gradient(
        owner, within, queries, prefix, out_grad[0], gain_row
    )
    suffix, back_owner = entering(block_grad, True)
    grad_q, wide_q = query_gradient(owner, d_att, values, keys, prefix, query_slope)

    dims = len(masks)
    orders = [tuple((start + i) % dims for i in range(dims)) for start in range(min(3, dims))]
    unit = features // 8
    cuts = [(0, 4 * unit), (4 * unit, 7 * unit), (7 * unit, 8 * unit)][: len(orders)]
    weight_q = scattered(x, grad_q, both_exchange(wide_q, 1), masks, orders, cuts)

    dk, dv = within_block(d_att, values, keys, queries)
    grad_k, wide_k, grad_v, wide_v = key_value_gradients(
        back_owner, dk, dv, values, keys, suffix, key_slope
    )
    weight_k = scattered(x, grad_k, both_exchange(wide_k, 1), masks, orders, cuts)
    weight_v = scattered(x, grad_v, both_exchange(wide_v, 1), masks, orders, cuts)

    input_grad = mm_nt(grad_q, w_query)
    input_grad = input_grad + mm_nt(grad_k, w_key)
    input_grad = input_grad + mm_nt(grad_v, w_value)
    resid_grad = input_grad.astype(BF16)[None]
    grad_scale = 1.0 / math.sqrt(positions * total)
    code_term = jnp.dot(code_values, input_grad, precision=lax.Precision.HIGHEST)
    small = jnp.concatenate([gain_term.reshape(-1), code_term.reshape(-1)]).reshape(-1, DH)
    small = sum_everywhere(small).reshape(-1) * grad_scale
    gain_sum, code_sum = small[:features], small[features:].reshape(code_term.shape)
    weights = jnp.stack([weight_q, weight_k, weight_v], axis=1) * grad_scale
    return resid_grad, weights, gain_sum, code_sum


def solution(mesh):
    return jax.shard_map(
        body,
        mesh=mesh,
        in_specs=(
            P("dp", "seq", None),
            P("dp", "seq"),
            P(),
            P(),
            P(),
            P(),
            P(),
            P("dp", "seq", None),
        ),
        out_specs=(P("dp", "seq", None), P(AXES, None, None), P(), P()),
        check_vma=False,
    )
```

```python
import functools
import math

import jax
import jax.numpy as jnp
from jax import lax
from jax.experimental import pallas as pl
from jax.experimental.pallas import tpu as pltpu
from jax.sharding import PartitionSpec as P

HEADS = 8
DH = 128
PAIR = 2
WIDE = PAIR * DH
PARTS = 2
SHARES = 2
AXES = ("seq", "dp")
F32 = jnp.float32
BF16 = jnp.bfloat16
MIB = 1024 * 1024
EMBED_MIB = 41

fsq_levels = (8, 8, 8, 5, 5, 5)
fsq_bases = (1, 8, 64, 512, 2560, 12800)

NT = (((1,), (1,)), ((), ()))
TN = (((0,), (0,)), ((), ()))
VMEM = pl.BlockSpec(memory_space=pltpu.VMEM)
SMEM = pl.BlockSpec(memory_space=pltpu.SMEM)
HBM = pl.BlockSpec(memory_space=pltpu.HBM)


def mm(a, b):
    return jnp.dot(a, b, preferred_element_type=F32)


def mm_nt(a, b):
    return lax.dot_general(a, b, NT, preferred_element_type=F32)


def mm_tn(a, b):
    return lax.dot_general(a, b, TN, preferred_element_type=F32)


def params(size):
    return pltpu.CompilerParams(vmem_limit_bytes=int(size) + 5 * MIB)


def cost(flops, moved):
    return pl.CostEstimate(flops=1, bytes_accessed=1, transcendentals=0)


def shape(dims, dtype):
    return jax.ShapeDtypeStruct(dims, dtype)


def silu_and_slope(value):
    sigma = 1.0 / (1.0 + jnp.exp(-value))
    return value * sigma, sigma * (1.0 + value * (1.0 - sigma))


def head(h):
    return slice(h * DH, (h + 1) * DH)


def part_rows(t, p):
    return slice(p * (t // PARTS), (p + 1) * (t // PARTS))


def hand_out(slot, part_sums, pieces):
    share = pieces[0].shape[0]
    for mask, piece in enumerate(pieces):
        heads = pl.ds((slot ^ mask) * share, share)
        total = part_sums[0, heads]
        for p in range(1, PARTS):
            total = total + part_sums[p, heads]
        piece[...] = total


def take_in(slot, pieces, out_ref):
    share = pieces[0].shape[0]
    for mask, piece in enumerate(pieces):
        out_ref[pl.ds((slot ^ mask) * share, share)] = piece[...]


def in_vmem(kernel, slots, inputs, outs, scratch, price, name):
    size = sum(math.prod(a.shape) * a.dtype.itemsize for a in [*inputs, *outs, *scratch])
    return pl.pallas_call(
        kernel,
        in_specs=[SMEM] * len(slots) + [VMEM] * len(inputs),
        out_specs=[VMEM] * len(outs),
        out_shape=outs,
        scratch_shapes=scratch,
        compiler_params=params(size),
        cost_estimate=price,
        name=name,
    )(*slots, *inputs)


def embed_kernel(
    slots, ids_hbm, proj_hbm, resid_hbm, wk_hbm, wv_hbm,
    x_ref, codes_ref, k_ref, slope_ref, v_ref, kv_ref, *rest,
):
    pieces = rest[:-6]
    ids_ref, proj_ref, resid_ref, wk_ref, wv_ref, sems = rest[-6:]
    t, d = x_ref.shape
    hd = k_ref.shape[1]
    half = hd // 2
    moves = [(ids_hbm, ids_ref), (proj_hbm, proj_ref), (resid_hbm, resid_ref)]
    for c in range(2):
        at = pl.ds(c * half, half)
        moves += [(wk_hbm.at[:, at], wk_ref.at[:, at]), (wv_hbm.at[:, at], wv_ref.at[:, at])]
    incoming = [pltpu.make_async_copy(hbm, ref, sems.at[i]) for i, (hbm, ref) in enumerate(moves)]
    for copy in incoming:
        copy.start()
    incoming[0].wait()
    ids = ids_ref[...]
    code_list = []
    for fsq_level, fsq_base in zip(fsq_levels, fsq_bases):
        digit = lax.rem(lax.div(ids, fsq_base), fsq_level)
        code_list.append((2.0 * digit.astype(F32) - (fsq_level - 1)) / (fsq_level - 1))
    count = len(code_list)
    for _ in range(codes_ref.shape[0] - count):
        code_list.append(jnp.zeros_like(code_list[0]))
    codes = jnp.concatenate(code_list, axis=0)
    codes_ref[...] = codes
    turned = jnp.transpose(codes)
    incoming[1].wait()
    incoming[2].wait()
    step = 64
    for r in range(0, t, step):
        summed = resid_ref[r : r + step].astype(F32)
        for index in range(count):
            summed = summed + turned[r : r + step, index : index + 1] * proj_ref[index : index + 1]
        x_ref[r : r + step] = summed.astype(BF16)
    x = x_ref[...]
    for c in range(2):
        at = slice(c * half, (c + 1) * half)
        incoming[3 + 2 * c].wait()
        key, slope = silu_and_slope(mm(x, wk_ref[:, at]))
        key = key.astype(BF16)
        k_ref[:, at] = key
        slope_ref[:, at] = slope
        incoming[4 + 2 * c].wait()
        value = mm(x, wv_ref[:, at]).astype(BF16)
        v_ref[:, at] = value
        for h in range(half // DH):
            for p in range(PARTS):
                rows = part_rows(t, p)
                kv_ref[p, c * (half // DH) + h] = mm_tn(key[rows, head(h)], value[rows, head(h)])
    hand_out(slots[0], kv_ref, pieces)


def embed_keys_values(slots, resid, token_ids, code_proj, w_key, w_value, group):
    t, d = resid.shape
    hd = w_key.shape[1]
    heads = hd // DH
    return pl.pallas_call(
        embed_kernel,
        in_specs=[SMEM] + [HBM] * 5,
        out_specs=[VMEM] * (6 + group),
        out_shape=[
            shape((t, d), BF16),
            shape((8, t), F32),
            shape((t, hd), BF16),
            shape((t, hd), F32),
            shape((t, hd), BF16),
            shape((PARTS, heads, DH, DH), F32),
        ]
        + [shape((heads // group, DH, DH), F32)] * group,
        scratch_shapes=[
            pltpu.VMEM(token_ids.shape, jnp.int32),
            pltpu.VMEM(code_proj.shape, F32),
            pltpu.VMEM((t, d), BF16),
            pltpu.VMEM((d, hd), BF16),
            pltpu.VMEM((d, hd), BF16),
            pltpu.SemaphoreType.DMA((7,)),
        ],
        compiler_params=params(EMBED_MIB * MIB),
        cost_estimate=cost(4 * t * d * hd, 4 * d * hd + 10 * t * hd),
        name="embed_keys_values",
    )(slots, token_ids, code_proj, resid, w_key, w_value)


def causal_mask(t, transposed):
    rows = lax.broadcasted_iota(jnp.int32, (t, t), 0)
    cols = lax.broadcasted_iota(jnp.int32, (t, t), 1)
    return rows <= cols if transposed else cols <= rows


def masked(mask, product):
    return jnp.where(mask, product, 0.0).astype(BF16)


def query_kernel(x_ref, wq_ref, k_ref, v_ref, q_ref, slope_ref, sv_ref):
    t = x_ref.shape[0]
    hd = q_ref.shape[1]
    half = hd // 2
    mask = causal_mask(t // PARTS, False)
    for c in range(2):
        at = slice(c * half, (c + 1) * half)
        query, slope = silu_and_slope(mm(x_ref[...], wq_ref[:, at]))
        query = query.astype(BF16)
        q_ref[:, at] = query
        slope_ref[:, at] = slope
        for h in range(half // DH):
            at = head(c * (half // DH) + h)
            for p in range(PARTS):
                rows = part_rows(t, p)
                scores = masked(mask, mm_nt(query[rows, head(h)], k_ref[rows, at]))
                sv_ref[rows, at] = mm(scores, v_ref[rows, at])


def queries_scores(x, w_query, keys, values):
    t, d = x.shape
    hd = w_query.shape[1]
    outs = [shape((t, hd), BF16), shape((t, hd), F32), shape((t, hd), F32)]
    price = cost(2 * t * d * hd + 2 * t * t * hd, 2 * d * hd + 14 * t * hd)
    return in_vmem(query_kernel, [], [x, w_query, keys, values], outs, [], price, "queries_scores")


def norm_kernel(slots, sv_ref, q_ref, kv_ref, og_ref, gain_ref, *rest):
    group = (len(rest) - 4) // 2
    prefixes, (datt_ref, term_ref, grad_ref), outs = rest[:group], rest[group : group + 3], rest[group + 3 : -1]
    state_ref = rest[-1]
    take_in(slots[0], prefixes, state_ref)
    t, hd = q_ref.shape
    for h in range(hd // DH):
        at = head(h)
        term = None
        state = state_ref[h]
        for p in range(PARTS):
            rows = part_rows(t, p)
            if p:
                state = state + kv_ref[p - 1, h]
            query = q_ref[rows, at]
            attended = sv_ref[rows, at] + mm(query, state.astype(BF16))
            inverse = lax.rsqrt(jnp.mean(attended * attended, axis=-1, keepdims=True) + 1e-06)
            normed = attended * inverse
            grad = og_ref[rows, at].astype(F32)
            more = jnp.sum(grad * normed, axis=0, keepdims=True)
            term = more if term is None else term + more
            d_normed = grad * gain_ref[:, at]
            inner = jnp.mean(d_normed * normed, axis=-1, keepdims=True)
            d_att = ((d_normed - normed * inner) * inverse).astype(BF16)
            datt_ref[rows, at] = d_att
            grad_ref[p, h] = mm_tn(query, d_att)
        term_ref[:, at] = term
    hand_out(slots[1], grad_ref, outs)


def norm_gradient(slots, sv, queries, prefixes, part_kv, out_grad, gain):
    t, hd = sv.shape
    heads = hd // DH
    group = len(prefixes)
    outs = [shape((t, hd), BF16), shape((1, hd), F32), shape((PARTS, heads, DH, DH), F32)]
    outs += [shape((heads // group, DH, DH), F32)] * group
    return in_vmem(
        norm_kernel, [slots], [sv, queries, part_kv, out_grad, gain, *prefixes], outs,
        [pltpu.VMEM((heads, DH, DH), F32)], cost(4 * t * hd * DH, 10 * t * hd), "norm_gradient",
    )


def store_wide(refs, rows, h, grad):
    width = refs[0].shape[1]
    start = h * DH % width
    refs[h * DH // width][rows, start : start + DH] = grad.astype(F32)


def dquery_kernel(slots, datt_ref, v_ref, k_ref, kv_ref, slope_ref, *rest):
    prefixes, (g16_ref, *wide, state_ref) = rest[: -2 - SHARES], rest[-2 - SHARES :]
    take_in(slots[0], prefixes, state_ref)
    t, hd = datt_ref.shape
    mask = causal_mask(t // PARTS, False)
    for h in range(hd // DH):
        at = head(h)
        state = state_ref[h]
        for p in range(PARTS):
            rows = part_rows(t, p)
            if p:
                state = state + kv_ref[p - 1, h]
            d_att = datt_ref[rows, at]
            back = masked(mask, mm_nt(d_att, v_ref[rows, at]))
            d_query = mm(back, k_ref[rows, at]) + mm_nt(d_att, state.astype(BF16))
            grad = (d_query * slope_ref[rows, at]).astype(BF16)
            g16_ref[rows, at] = grad
            store_wide(wide, rows, h, grad)


def query_gradient(slots, d_att, values, keys, prefixes, part_kv, slope):
    t, hd = d_att.shape
    return in_vmem(
        dquery_kernel, [slots], [d_att, values, keys, part_kv, slope, *prefixes],
        [shape((t, hd), BF16)] + [shape((t, hd // SHARES), F32)] * SHARES, [pltpu.VMEM((hd // DH, DH, DH), F32)],
        cost(2 * t * t * hd, 16 * t * hd), "query_gradient",
    )


def within_kernel(datt_ref, v_ref, k_ref, q_ref, dk_ref, dv_ref):
    t, hd = datt_ref.shape
    mask = causal_mask(t // PARTS, True)
    for h in range(hd // DH):
        at = head(h)
        for p in range(PARTS):
            rows = part_rows(t, p)
            d_att, query = datt_ref[rows, at], q_ref[rows, at]
            back = masked(mask, mm_nt(v_ref[rows, at], d_att))
            dk_ref[rows, at] = mm(back, query)
            scores = masked(mask, mm_nt(k_ref[rows, at], query))
            dv_ref[rows, at] = mm(scores, d_att)


def within_block(d_att, values, keys, queries):
    t, hd = d_att.shape
    return in_vmem(
        within_kernel, [], [d_att, values, keys, queries], [shape((t, hd), F32)] * 2, [],
        cost(4 * t * t * hd, 16 * t * hd), "within_block",
    )


def dkv_kernel(slots, dk_ref, dv_ref, v_ref, k_ref, grad_ref, slope_ref, *rest):
    suffixes, outs, state_ref = rest[: -3 - 2 * SHARES], rest[-3 - 2 * SHARES : -1], rest[-1]
    (k16, *wide_k), (v16, *wide_v) = outs[: 1 + SHARES], outs[1 + SHARES :]
    take_in(slots[1], suffixes, state_ref)
    t, hd = dk_ref.shape
    for h in range(hd // DH):
        at = head(h)
        state = state_ref[h]
        for p in reversed(range(PARTS)):
            rows = part_rows(t, p)
            if p < PARTS - 1:
                state = state + grad_ref[p + 1, h]
            suffix = state.astype(BF16)
            d_key = dk_ref[rows, at] + mm_nt(v_ref[rows, at], suffix)
            grad = (d_key * slope_ref[rows, at]).astype(BF16)
            k16[rows, at] = grad
            store_wide(wide_k, rows, h, grad)
            grad = (dv_ref[rows, at] + mm(k_ref[rows, at], suffix)).astype(BF16)
            v16[rows, at] = grad
            store_wide(wide_v, rows, h, grad)


def key_value_gradients(slots, dk, dv, values, keys, suffixes, part_grad, slope):
    t, hd = dk.shape
    return in_vmem(
        dkv_kernel, [slots], [dk, dv, values, keys, part_grad, slope, *suffixes],
        ([shape((t, hd), BF16)] + [shape((t, hd // SHARES), F32)] * SHARES) * 2,
        [pltpu.VMEM((hd // DH, DH, DH), F32)],
        cost(4 * t * hd * DH, 28 * t * hd), "key_value_gradients",
    )


class Order:
    def __init__(self):
        self.last = None

    def tied(self, *arrays):
        if self.last is not None:
            *arrays, _ = lax.optimization_barrier((*arrays, self.last))
        return arrays[0] if len(arrays) == 1 else tuple(arrays)

    def mark(self, array):
        self.last = array


def exchange(array, axis, mask):
    count = lax.axis_size(axis)
    return lax.ppermute(array, axis, [(i, i ^ mask) for i in range(count)])


def combine_kernel(inner, base_ref, *refs):
    group = len(refs) // 2
    blocks, outs = refs[:group], refs[group:]
    for mask, out_ref in enumerate(outs):
        out_ref[...] = base_ref[...]
        for other, block in enumerate(blocks):
            if other != mask:

                @pl.when((inner[0] ^ other) < (inner[0] ^ mask))
                def _(out_ref=out_ref, block=block):
                    out_ref[...] += block[...]


def combine(inner, base, blocks):
    outs = [shape(base.shape, F32)] * len(blocks)
    return list(in_vmem(combine_kernel, [inner], [base, *blocks], outs, [], cost(0, 0), "combine"))


class Entering:
    def __init__(self, reverse):
        self.reverse = reverse
        self.count = lax.axis_size("seq")
        self.group = min(HEADS // PAIR, self.count)
        place = lax.axis_index("seq")
        if reverse:
            place = self.count - 1 - place
        self.inner, cluster = place % self.group, place // self.group
        self.twist = self.group // 2
        self.slot = (self.inner ^ (self.twist * (cluster % 2))).astype(jnp.int32)
        self.inner = self.inner.astype(jnp.int32)

    def first(self, pieces):
        self.blocks = [pieces[0]]
        for mask in range(1, self.group):
            self.blocks.append(exchange(pieces[mask], "seq", mask))

    def second(self, order):
        self.blocks[1:] = order.tied(*self.blocks[1:])
        total = sum(self.blocks[1:], self.blocks[0])
        order.mark(total)
        group, twist, count = self.group, self.twist, self.count
        clusters = count // group
        self.bases = []
        for shift in range(1, clusters):
            pairs = []
            for source in range(clusters - shift):
                for slot in range(group):
                    a = source * group + (slot ^ (twist * (source % 2)))
                    target = source + shift
                    b = target * group + (slot ^ (twist * (target % 2)))
                    pairs.append((count - 1 - a, count - 1 - b) if self.reverse else (a, b))
            self.bases.append(lax.ppermute(total, "seq", pairs))

    def third(self, order):
        bases = order.tied(*self.bases)
        if len(self.bases) == 1:
            bases = (bases,)
        base = sum(bases[1:], bases[0])
        self.outs = combine(self.inner, base, self.blocks)
        order.mark(self.outs[0])
        for mask in range(1, self.group):
            self.outs[mask] = exchange(self.outs[mask], "seq", mask)

    def result(self, order):
        self.outs[1:] = order.tied(*self.outs[1:])
        return self.outs


def both_exchange(array, masks):
    total = lax.axis_size("seq") * lax.axis_size("dp")
    return lax.ppermute(array, AXES, [(i, i ^ masks[i % 2]) for i in range(total)])


def turn_kernel(me_ref, x_ref, own_ref, other_ref, turned_ref):
    chips, rows, t = own_ref.shape
    core, chip = me_ref[0] % 2, me_ref[0] // 2
    span = 128 // (2 * rows)
    for block in range(chips // span):
        turned_ref[block] = jnp.transpose(x_ref[:, block * 128 : (block + 1) * 128])
    for block in range(chips // span):
        for i in range(span):
            slot = (block * span + i) ^ chip
            mine = pl.multiple_of((2 * i + core) * rows, rows)
            theirs = pl.multiple_of((2 * i + 1 - core) * rows, rows)
            own_ref[slot] = turned_ref[block, pl.ds(mine, rows)]
            other_ref[slot] = turned_ref[block, pl.ds(theirs, rows)].astype(F32)


def turn(me, x, chips):
    t, d = x.shape
    rows = d // (2 * chips)
    return in_vmem(
        turn_kernel, [me], [x], [shape((chips, rows, t), BF16), shape((chips, rows, t), F32)],
        [pltpu.VMEM((d // 128, 128, t), BF16)], cost(0, 12 * t * d), "turn_inputs",
    )


def merge_kernel(own_ref, other_ref, out_ref):
    half = own_ref.shape[-1]
    out_ref[:, :, :half] = own_ref[...]
    out_ref[:, :, half:] = other_ref[...].astype(BF16)


def merge(own, other):
    chips, rows, t = own.shape
    outs = [shape((chips, rows, 2 * t), BF16)]
    return in_vmem(merge_kernel, [], [own, other], outs, [], cost(0, 10 * own.size), "merge_inputs")[0]


def product_kernel(parts, me_ref, x_ref, own_ref, *rest):
    other_refs, out_refs = rest[: -len(parts)], rest[-len(parts) :]
    core = me_ref[0] % 2
    other = jnp.concatenate([ref[...].astype(BF16) for ref in other_refs], axis=1)
    for out_ref, (slots, start, stop) in zip(out_refs, parts):
        grads = jnp.concatenate([own_ref[:, start:stop], other[:, start:stop]], axis=0)
        rows = jnp.concatenate([x_ref[a ^ (core * (a ^ b))] for a, b in slots], axis=0)
        out_ref[...] = mm(rows, grads)


def products(me, x, own, others, parts, name):
    rows = x.shape[1]
    outs = [shape((len(slots) * rows, stop - start), F32) for slots, start, stop in parts]
    kernel = functools.partial(product_kernel, parts)
    return in_vmem(kernel, [me], [x, own, *others], outs, [], cost(0, 0), name)


class Chunk:
    def __init__(self, start, stop, orders, masks):
        self.start, self.stop = start, stop
        self.orders = [[masks[axis] for axis in order] for order in orders]
        self.step = 0

    def slots(self, sent):
        out = []
        for masks in self.orders:
            mine = []
            for pick in range(1 << (len(masks) - 1)):
                slot = masks[0] >> 1 if sent else 0
                for place, mask in enumerate(masks[1:]):
                    if pick >> (len(masks) - 2 - place) & 1:
                        slot ^= mask >> 1
                mine.append(slot)
            out.append(mine)
        return tuple(zip(*out))

    def masks(self, step):
        return [masks[step] for masks in self.orders]

    def launch(self, sending):
        self.got = both_exchange(sending, self.masks(self.step))
        self.step += 1

    def advance(self, order, small=None):
        rest, got = self.rest, order.tied(self.got)
        extra = got.shape[0] - rest.shape[0]
        if self.step == len(self.orders[0]):
            self.rest = None
            if extra:
                self.out, small = add_last(rest, got, small)
                order.mark(small)
                return small
            self.out = rest + got
            order.mark(got)
            return None
        half = rest.shape[0] // 2
        if small is None:
            sending = add_rows(rest, got, half, half)
        else:
            sending, small = add_rows_with(rest, got, small)
        order.mark(sending)
        self.launch(sending)
        self.rest = add_rows(rest, order.tied(got), 0, half)
        order.mark(self.rest)
        return small


def add_kernel(start, a_ref, b_ref, out_ref):
    rows = slice(start, start + out_ref.shape[0])
    out_ref[...] = a_ref[rows] + b_ref[rows]


def add_rows(a, b, start, rows):
    outs = [shape((rows, a.shape[1]), F32)]
    kernel = functools.partial(add_kernel, start)
    return in_vmem(kernel, [], [a, b], outs, [], cost(0, 0), "add_rows")[0]


def add_with_kernel(rest_ref, got_ref, small_ref, sending_ref, sum_ref):
    full = rest_ref.shape[0]
    half = full // 2
    total = small_ref[...]
    if got_ref.shape[0] > full:
        total = total + got_ref[full:]
    sum_ref[...] = total
    sending_ref[half:] = total
    sending_ref[:half] = rest_ref[half:] + got_ref[half:full]


def add_rows_with(rest, got, small):
    outs = [shape((rows, rest.shape[1]), F32) for rows in (rest.shape[0] // 2 + small.shape[0], small.shape[0])]
    return in_vmem(add_with_kernel, [], [rest, got, small], outs, [], cost(0, 0), "add_rows_with")


def add_last_kernel(rest_ref, got_ref, small_ref, out_ref, sum_ref):
    full = rest_ref.shape[0]
    out_ref[...] = rest_ref[...] + got_ref[:full]
    sum_ref[...] = small_ref[...] + got_ref[full:]


def add_last(rest, got, small):
    outs = [shape(rest.shape, F32), shape(small.shape, F32)]
    return in_vmem(add_last_kernel, [], [rest, got, small], outs, [], cost(0, 0), "add_last")


def first_input_kernel(grad_ref, w_ref, out_ref):
    out_ref[...] = mm_nt(grad_ref[...], w_ref[...])


def rest_input_kernel(first_ref, codes_ref, grad_a, grad_b, wa_ref, wb_ref, out_ref, term_ref):
    total = first_ref[...] + mm_nt(grad_a[...], wa_ref[...]) + mm_nt(grad_b[...], wb_ref[...])
    out_ref[...] = total.astype(BF16)
    term_ref[...] = jnp.dot(
        codes_ref[...], total, precision=lax.Precision.HIGHEST, preferred_element_type=F32
    )


def row_blocks(w):
    return pl.BlockSpec((WIDE, w.shape[1]), lambda i: (i, 0))


def out_columns(rows):
    return pl.BlockSpec((rows, WIDE), lambda i: (0, i))


def first_input_gradient(grad, w):
    t, d = grad.shape[0], w.shape[0]
    return pl.pallas_call(
        first_input_kernel,
        grid=(d // WIDE,),
        in_specs=[VMEM, row_blocks(w)],
        out_specs=out_columns(t),
        out_shape=shape((t, d), F32),
        compiler_params=params(4 * t * WIDE * 4 + 4 * WIDE * w.shape[1] + 2 * grad.size),
        cost_estimate=cost(0, 0),
        name="input_gradient_q",
    )(grad, w)


def rest_input_gradient(first, codes, grad_a, grad_b, wa, wb):
    t, d = first.shape
    rows = codes.shape[0]
    size = 8 * t * WIDE * 4 + 8 * WIDE * wa.shape[1] + 4 * grad_a.size
    return pl.pallas_call(
        rest_input_kernel,
        grid=(d // WIDE,),
        in_specs=[out_columns(t), VMEM, VMEM, VMEM, row_blocks(wa), row_blocks(wb)],
        out_specs=[out_columns(t), out_columns(rows)],
        out_shape=[shape((t, d), BF16), shape((rows, d), F32)],
        compiler_params=params(size),
        cost_estimate=cost(0, 0),
        name="input_gradient_kv",
    )(first, codes, grad_a, grad_b, wa, wb)


def body(resid, token_ids, code_proj, w_query, w_key, w_value, gain, out_grad):
    positions, width = resid.shape[1:]
    features = w_query.shape[1]
    n_dp = lax.axis_size("dp")
    total = lax.axis_size("seq") * n_dp
    me = (lax.axis_index("seq") * n_dp + lax.axis_index("dp")).astype(jnp.int32).reshape(1)
    order = Order()

    before, after = Entering(False), Entering(True)
    slots = jnp.stack([before.slot, after.slot])
    before.inner, after.inner = before.inner.reshape(1), after.inner.reshape(1)
    slots, me, before.inner, after.inner = lax.optimization_barrier((slots, me, before.inner, after.inner))
    x, code_values, keys, key_slope, values, part_kv, *pieces = embed_keys_values(
        slots, resid[0], token_ids, code_proj, w_key, w_value, before.group
    )
    before.first(pieces)
    queries, query_slope, within = queries_scores(x, w_query, keys, values)
    order.mark(within)
    before.second(order)
    own_rows, other_rows = turn(me, order.tied(x), total // 2)
    order.mark(own_rows)
    other_rows = both_exchange(other_rows, (1, 1))
    before.third(order)
    prefixes = before.result(order)

    d_att, gain_term, part_grad, *pieces = norm_gradient(
        slots, within, queries, prefixes, part_kv, out_grad[0], gain.reshape(1, features)
    )
    order.mark(d_att)
    after.first(pieces)
    grad_q, *wide_q = query_gradient(slots, order.tied(d_att), values, keys, prefixes, part_kv, query_slope)
    order.mark(grad_q)
    wide_q = [both_exchange(share, (1, 1)) for share in wide_q]
    merged = merge(own_rows, order.tied(other_rows))
    order.mark(merged)
    after.second(order)

    bits = total.bit_length() - 1
    masks = [1 << b for b in range(1, bits)]
    masks[-1] |= masks[-2]
    dims = len(masks)

    unit = features // 8
    extra = tuple(range(4, dims))

    def chunks_of(plan):
        out, start = [], 0
        for units, *orders in plan:
            axes = [tuple("xyzw".index(name) for name in order) + extra for order in orders]
            out.append(Chunk(start * unit, (start + units) * unit, axes, masks))
            start += units
        return out

    chunks_q = chunks_of([(8, "yxzw", "xyzw")])
    chunks_k = chunks_of([(8, "zyxw", "zxyw")])
    chunks_v = chunks_of([(8, "yxzw", "xzyw")])
    every = chunks_q + chunks_k + chunks_v

    def begin(chunks, own, others, name):
        own, *others = order.tied(own, *others)
        sent = products(me, merged, own, others, [(c.slots(True), c.start, c.stop) for c in chunks], name)
        order.mark(sent[0])
        for chunk, array in zip(chunks, sent):
            chunk.launch(array)
        kept = products(me, merged, order.tied(own), others, [(c.slots(False), c.start, c.stop) for c in chunks], name + "_kept")
        order.mark(kept[0])
        for chunk, array in zip(chunks, kept):
            chunk.rest = array

    begin(chunks_q, grad_q, wide_q, "weight_q")
    dk, dv = within_block(order.tied(d_att), values, keys, queries)
    order.mark(dk)
    after.third(order)
    input_grad = first_input_gradient(order.tied(grad_q), w_query)
    order.mark(input_grad)
    suffixes = after.result(order)
    outs = key_value_gradients(slots, dk, dv, values, keys, suffixes, part_grad, key_slope)
    (grad_k, *wide_k), (grad_v, *wide_v) = outs[: 1 + SHARES], outs[1 + SHARES :]
    order.mark(grad_k)
    wide_k = [both_exchange(share, (1, 1)) for share in wide_k]
    wide_v = [both_exchange(share, (1, 1)) for share in wide_v]
    begin(chunks_k, grad_k, wide_k, "weight_k")
    begin(chunks_v, grad_v, wide_v, "weight_v")
    resid_grad, code_term = rest_input_gradient(
        input_grad, code_values, order.tied(grad_k), grad_v, w_key, w_value
    )
    order.mark(code_term)
    grad_scale = 1.0 / math.sqrt(positions * total)
    codes = len(fsq_levels)
    carrier = chunks_q[0]
    edge = carrier.stop - carrier.start
    small = jnp.concatenate([gain_term.reshape(-1), code_term[:codes].reshape(-1)])
    used = small.shape[0]
    small = jnp.pad(small, (0, -used % (8 * edge))).reshape(-1, edge)

    def advance(index):
        nonlocal small
        if every[index] is carrier:
            small = carrier.advance(order, small)
        else:
            every[index].advance(order)

    small = small + order.tied(both_exchange(small, (1, 1)))
    order.mark(small)
    for index in (0, 2, 0, 1, 2, 0, 1):
        advance(index)
    while any(c.step < dims for c in every):
        for index, c in enumerate(every):
            if c.step < dims:
                advance(index)
    advance(0)
    small = small + order.tied(both_exchange(small, carrier.masks(0)))
    order.mark(small)
    for index in (2, 1):
        advance(index)
    small = small.reshape(-1)[:used] * grad_scale
    gain_sum, code_sum = small[:features], small[features:].reshape(codes, width)

    def joined(chunks):
        return jnp.concatenate([c.out for c in chunks], axis=-1)

    weights = jnp.stack([joined(chunks_q), joined(chunks_k), joined(chunks_v)], axis=1) * grad_scale
    return resid_grad[None], weights, gain_sum, code_sum


def solution(mesh):
    return jax.shard_map(
        body,
        mesh=mesh,
        in_specs=(
            P("dp", "seq", None),
            P("dp", "seq"),
            P(),
            P(),
            P(),
            P(),
            P(),
            P("dp", "seq", None),
        ),
        out_specs=(P("dp", "seq", None), P(AXES, None, None), P(), P()),
        check_vma=False,
    )
```

```python
import functools
import math

import jax
import jax.numpy as jnp
from jax import lax
from jax.experimental import pallas as pl
from jax.experimental.pallas import tpu as pltpu
from jax.sharding import PartitionSpec as P

HEADS = 8
DH = 128
PAIR = 2
WIDE = PAIR * DH
PARTS = 2
SHARES = 2
AXES = ("seq", "dp")
F32 = jnp.float32
BF16 = jnp.bfloat16
MIB = 1024 * 1024
EMBED_MIB = 41

fsq_levels = (8, 8, 8, 5, 5, 5)
fsq_bases = (1, 8, 64, 512, 2560, 12800)

NT = (((1,), (1,)), ((), ()))
TN = (((0,), (0,)), ((), ()))
VMEM = pl.BlockSpec(memory_space=pltpu.VMEM)
SMEM = pl.BlockSpec(memory_space=pltpu.SMEM)
HBM = pl.BlockSpec(memory_space=pltpu.HBM)


def mm(a, b):
    return jnp.dot(a, b, preferred_element_type=F32)


def mm_nt(a, b):
    return lax.dot_general(a, b, NT, preferred_element_type=F32)


def mm_tn(a, b):
    return lax.dot_general(a, b, TN, preferred_element_type=F32)


def params(size):
    return pltpu.CompilerParams(vmem_limit_bytes=int(size) + 5 * MIB)


def cost(flops, moved):
    return pl.CostEstimate(flops=1, bytes_accessed=1, transcendentals=0)


def shape(dims, dtype):
    return jax.ShapeDtypeStruct(dims, dtype)


def silu_and_slope(value):
    sigma = 1.0 / (1.0 + jnp.exp(-value))
    return value * sigma, sigma * (1.0 + value * (1.0 - sigma))


def head(h):
    return slice(h * DH, (h + 1) * DH)


def part_rows(t, p):
    return slice(p * (t // PARTS), (p + 1) * (t // PARTS))


def hand_out(slot, part_sums, pieces):
    share = pieces[0].shape[0]
    for mask, piece in enumerate(pieces):
        heads = pl.ds((slot ^ mask) * share, share)
        total = part_sums[0, heads]
        for p in range(1, PARTS):
            total = total + part_sums[p, heads]
        piece[...] = total


def take_in(slot, pieces, out_ref):
    share = pieces[0].shape[0]
    for mask, piece in enumerate(pieces):
        out_ref[pl.ds((slot ^ mask) * share, share)] = piece[...]


def in_vmem(kernel, slots, inputs, outs, scratch, price, name):
    size = sum(math.prod(a.shape) * a.dtype.itemsize for a in [*inputs, *outs, *scratch])
    return pl.pallas_call(
        kernel,
        in_specs=[SMEM] * len(slots) + [VMEM] * len(inputs),
        out_specs=[VMEM] * len(outs),
        out_shape=outs,
        scratch_shapes=scratch,
        compiler_params=params(size),
        cost_estimate=price,
        name=name,
    )(*slots, *inputs)


def embed_kernel(
    slots, ids_hbm, proj_hbm, resid_hbm, wk_hbm, wv_hbm,
    x_ref, codes_ref, k_ref, slope_ref, v_ref, kv_ref, *rest,
):
    pieces = rest[:-6]
    ids_ref, proj_ref, resid_ref, wk_ref, wv_ref, sems = rest[-6:]
    t, d = x_ref.shape
    hd = k_ref.shape[1]
    half = hd // 2
    moves = [(ids_hbm, ids_ref), (proj_hbm, proj_ref), (resid_hbm, resid_ref)]
    for c in range(2):
        at = pl.ds(c * half, half)
        moves += [(wk_hbm.at[:, at], wk_ref.at[:, at]), (wv_hbm.at[:, at], wv_ref.at[:, at])]
    incoming = [pltpu.make_async_copy(hbm, ref, sems.at[i]) for i, (hbm, ref) in enumerate(moves)]
    for copy in incoming:
        copy.start()
    incoming[0].wait()
    ids = ids_ref[...]
    code_list = []
    for fsq_level, fsq_base in zip(fsq_levels, fsq_bases):
        digit = lax.rem(lax.div(ids, fsq_base), fsq_level)
        code_list.append((2.0 * digit.astype(F32) - (fsq_level - 1)) / (fsq_level - 1))
    count = len(code_list)
    for _ in range(codes_ref.shape[0] - count):
        code_list.append(jnp.zeros_like(code_list[0]))
    codes = jnp.concatenate(code_list, axis=0)
    codes_ref[...] = codes
    turned = jnp.transpose(codes)
    incoming[1].wait()
    incoming[2].wait()
    step = 64
    for r in range(0, t, step):
        summed = resid_ref[r : r + step].astype(F32)
        for index in range(count):
            summed = summed + turned[r : r + step, index : index + 1] * proj_ref[index : index + 1]
        x_ref[r : r + step] = summed.astype(BF16)
    x = x_ref[...]
    for c in range(2):
        at = slice(c * half, (c + 1) * half)
        incoming[3 + 2 * c].wait()
        key, slope = silu_and_slope(mm(x, wk_ref[:, at]))
        key = key.astype(BF16)
        k_ref[:, at] = key
        slope_ref[:, at] = slope
        incoming[4 + 2 * c].wait()
        value = mm(x, wv_ref[:, at]).astype(BF16)
        v_ref[:, at] = value
        for h in range(half // DH):
            for p in range(PARTS):
                rows = part_rows(t, p)
                kv_ref[p, c * (half // DH) + h] = mm_tn(key[rows, head(h)], value[rows, head(h)])
    hand_out(slots[0], kv_ref, pieces)


def embed_keys_values(slots, resid, token_ids, code_proj, w_key, w_value, group):
    t, d = resid.shape
    hd = w_key.shape[1]
    heads = hd // DH
    return pl.pallas_call(
        embed_kernel,
        in_specs=[SMEM] + [HBM] * 5,
        out_specs=[VMEM] * (6 + group),
        out_shape=[
            shape((t, d), BF16),
            shape((8, t), F32),
            shape((t, hd), BF16),
            shape((t, hd), F32),
            shape((t, hd), BF16),
            shape((PARTS, heads, DH, DH), F32),
        ]
        + [shape((heads // group, DH, DH), F32)] * group,
        scratch_shapes=[
            pltpu.VMEM(token_ids.shape, jnp.int32),
            pltpu.VMEM(code_proj.shape, F32),
            pltpu.VMEM((t, d), BF16),
            pltpu.VMEM((d, hd), BF16),
            pltpu.VMEM((d, hd), BF16),
            pltpu.SemaphoreType.DMA((7,)),
        ],
        compiler_params=params(EMBED_MIB * MIB),
        cost_estimate=cost(4 * t * d * hd, 4 * d * hd + 10 * t * hd),
        name="embed_keys_values",
    )(slots, token_ids, code_proj, resid, w_key, w_value)


def causal_mask(t, transposed):
    rows = lax.broadcasted_iota(jnp.int32, (t, t), 0)
    cols = lax.broadcasted_iota(jnp.int32, (t, t), 1)
    return rows <= cols if transposed else cols <= rows


def masked(mask, product):
    return jnp.where(mask, product, 0.0).astype(BF16)


def query_kernel(x_ref, wq_ref, k_ref, v_ref, q_ref, slope_ref, sv_ref):
    t = x_ref.shape[0]
    hd = q_ref.shape[1]
    half = hd // 2
    mask = causal_mask(t // PARTS, False)
    for c in range(2):
        at = slice(c * half, (c + 1) * half)
        query, slope = silu_and_slope(mm(x_ref[...], wq_ref[:, at]))
        query = query.astype(BF16)
        q_ref[:, at] = query
        slope_ref[:, at] = slope
        for h in range(half // DH):
            at = head(c * (half // DH) + h)
            for p in range(PARTS):
                rows = part_rows(t, p)
                scores = masked(mask, mm_nt(query[rows, head(h)], k_ref[rows, at]))
                sv_ref[rows, at] = mm(scores, v_ref[rows, at])


def queries_scores(x, w_query, keys, values):
    t, d = x.shape
    hd = w_query.shape[1]
    outs = [shape((t, hd), BF16), shape((t, hd), F32), shape((t, hd), F32)]
    price = cost(2 * t * d * hd + 2 * t * t * hd, 2 * d * hd + 14 * t * hd)
    return in_vmem(query_kernel, [], [x, w_query, keys, values], outs, [], price, "queries_scores")


def norm_kernel(slots, sv_ref, q_ref, kv_ref, og_ref, gain_ref, *rest):
    group = (len(rest) - 4) // 2
    prefixes, (datt_ref, term_ref, grad_ref), outs = rest[:group], rest[group : group + 3], rest[group + 3 : -1]
    state_ref = rest[-1]
    take_in(slots[0], prefixes, state_ref)
    t, hd = q_ref.shape
    for h in range(hd // DH):
        at = head(h)
        term = None
        state = state_ref[h]
        for p in range(PARTS):
            rows = part_rows(t, p)
            if p:
                state = state + kv_ref[p - 1, h]
            query = q_ref[rows, at]
            attended = sv_ref[rows, at] + mm(query, state.astype(BF16))
            inverse = lax.rsqrt(jnp.mean(attended * attended, axis=-1, keepdims=True) + 1e-06)
            normed = attended * inverse
            grad = og_ref[rows, at].astype(F32)
            more = jnp.sum(grad * normed, axis=0, keepdims=True)
            term = more if term is None else term + more
            d_normed = grad * gain_ref[:, at]
            inner = jnp.mean(d_normed * normed, axis=-1, keepdims=True)
            d_att = ((d_normed - normed * inner) * inverse).astype(BF16)
            datt_ref[rows, at] = d_att
            grad_ref[p, h] = mm_tn(query, d_att)
        term_ref[:, at] = term
    hand_out(slots[1], grad_ref, outs)


def norm_gradient(slots, sv, queries, prefixes, part_kv, out_grad, gain):
    t, hd = sv.shape
    heads = hd // DH
    group = len(prefixes)
    outs = [shape((t, hd), BF16), shape((1, hd), F32), shape((PARTS, heads, DH, DH), F32)]
    outs += [shape((heads // group, DH, DH), F32)] * group
    return in_vmem(
        norm_kernel, [slots], [sv, queries, part_kv, out_grad, gain, *prefixes], outs,
        [pltpu.VMEM((heads, DH, DH), F32)], cost(4 * t * hd * DH, 10 * t * hd), "norm_gradient",
    )


def store_wide(refs, rows, h, grad):
    width = refs[0].shape[1]
    start = h * DH % width
    refs[h * DH // width][rows, start : start + DH] = grad.astype(F32)


def dquery_kernel(slots, datt_ref, v_ref, k_ref, kv_ref, slope_ref, *rest):
    prefixes, (g16_ref, *wide, state_ref) = rest[: -2 - SHARES], rest[-2 - SHARES :]
    take_in(slots[0], prefixes, state_ref)
    t, hd = datt_ref.shape
    mask = causal_mask(t // PARTS, False)
    for h in range(hd // DH):
        at = head(h)
        state = state_ref[h]
        for p in range(PARTS):
            rows = part_rows(t, p)
            if p:
                state = state + kv_ref[p - 1, h]
            d_att = datt_ref[rows, at]
            back = masked(mask, mm_nt(d_att, v_ref[rows, at]))
            d_query = mm(back, k_ref[rows, at]) + mm_nt(d_att, state.astype(BF16))
            grad = (d_query * slope_ref[rows, at]).astype(BF16)
            g16_ref[rows, at] = grad
            store_wide(wide, rows, h, grad)


def query_gradient(slots, d_att, values, keys, prefixes, part_kv, slope):
    t, hd = d_att.shape
    return in_vmem(
        dquery_kernel, [slots], [d_att, values, keys, part_kv, slope, *prefixes],
        [shape((t, hd), BF16)] + [shape((t, hd // SHARES), F32)] * SHARES, [pltpu.VMEM((hd // DH, DH, DH), F32)],
        cost(2 * t * t * hd, 16 * t * hd), "query_gradient",
    )


def within_kernel(datt_ref, v_ref, k_ref, q_ref, dk_ref, dv_ref):
    t, hd = datt_ref.shape
    mask = causal_mask(t // PARTS, True)
    for h in range(hd // DH):
        at = head(h)
        for p in range(PARTS):
            rows = part_rows(t, p)
            d_att, query = datt_ref[rows, at], q_ref[rows, at]
            back = masked(mask, mm_nt(v_ref[rows, at], d_att))
            dk_ref[rows, at] = mm(back, query)
            scores = masked(mask, mm_nt(k_ref[rows, at], query))
            dv_ref[rows, at] = mm(scores, d_att)


def within_block(d_att, values, keys, queries):
    t, hd = d_att.shape
    return in_vmem(
        within_kernel, [], [d_att, values, keys, queries], [shape((t, hd), F32)] * 2, [],
        cost(4 * t * t * hd, 16 * t * hd), "within_block",
    )


def dkv_kernel(slots, dk_ref, dv_ref, v_ref, k_ref, grad_ref, slope_ref, *rest):
    suffixes, outs, state_ref = rest[: -3 - 2 * SHARES], rest[-3 - 2 * SHARES : -1], rest[-1]
    (k16, *wide_k), (v16, *wide_v) = outs[: 1 + SHARES], outs[1 + SHARES :]
    take_in(slots[1], suffixes, state_ref)
    t, hd = dk_ref.shape
    for h in range(hd // DH):
        at = head(h)
        state = state_ref[h]
        for p in reversed(range(PARTS)):
            rows = part_rows(t, p)
            if p < PARTS - 1:
                state = state + grad_ref[p + 1, h]
            suffix = state.astype(BF16)
            d_key = dk_ref[rows, at] + mm_nt(v_ref[rows, at], suffix)
            grad = (d_key * slope_ref[rows, at]).astype(BF16)
            k16[rows, at] = grad
            store_wide(wide_k, rows, h, grad)
            grad = (dv_ref[rows, at] + mm(k_ref[rows, at], suffix)).astype(BF16)
            v16[rows, at] = grad
            store_wide(wide_v, rows, h, grad)


def key_value_gradients(slots, dk, dv, values, keys, suffixes, part_grad, slope):
    t, hd = dk.shape
    return in_vmem(
        dkv_kernel, [slots], [dk, dv, values, keys, part_grad, slope, *suffixes],
        ([shape((t, hd), BF16)] + [shape((t, hd // SHARES), F32)] * SHARES) * 2,
        [pltpu.VMEM((hd // DH, DH, DH), F32)],
        cost(4 * t * hd * DH, 28 * t * hd), "key_value_gradients",
    )


class Order:
    def __init__(self):
        self.last = None

    def tied(self, *arrays):
        if self.last is not None:
            *arrays, _ = lax.optimization_barrier((*arrays, self.last))
        return arrays[0] if len(arrays) == 1 else tuple(arrays)

    def mark(self, array):
        self.last = array


def exchange(array, axis, mask):
    count = lax.axis_size(axis)
    return lax.ppermute(array, axis, [(i, i ^ mask) for i in range(count)])


def combine_kernel(inner, base_ref, *refs):
    group = len(refs) // 2
    blocks, outs = refs[:group], refs[group:]
    for mask, out_ref in enumerate(outs):
        out_ref[...] = base_ref[...]
        for other, block in enumerate(blocks):
            if other != mask:

                @pl.when((inner[0] ^ other) < (inner[0] ^ mask))
                def _(out_ref=out_ref, block=block):
                    out_ref[...] += block[...]


def combine(inner, base, blocks):
    outs = [shape(base.shape, F32)] * len(blocks)
    return list(in_vmem(combine_kernel, [inner], [base, *blocks], outs, [], cost(0, 0), "combine"))


class Entering:
    def __init__(self, reverse):
        self.reverse = reverse
        self.count = lax.axis_size("seq")
        self.group = min(HEADS // PAIR, self.count)
        place = lax.axis_index("seq")
        if reverse:
            place = self.count - 1 - place
        self.inner, cluster = place % self.group, place // self.group
        self.twist = self.group // 2
        self.slot = (self.inner ^ (self.twist * (cluster % 2))).astype(jnp.int32)
        self.inner = self.inner.astype(jnp.int32)

    def first(self, pieces):
        self.blocks = [pieces[0]]
        for mask in range(1, self.group):
            self.blocks.append(exchange(pieces[mask], "seq", mask))

    def second(self, order):
        self.blocks[1:] = order.tied(*self.blocks[1:])
        total = sum(self.blocks[1:], self.blocks[0])
        order.mark(total)
        group, twist, count = self.group, self.twist, self.count
        clusters = count // group
        self.bases = []
        for shift in range(1, clusters):
            pairs = []
            for source in range(clusters - shift):
                for slot in range(group):
                    a = source * group + (slot ^ (twist * (source % 2)))
                    target = source + shift
                    b = target * group + (slot ^ (twist * (target % 2)))
                    pairs.append((count - 1 - a, count - 1 - b) if self.reverse else (a, b))
            self.bases.append(lax.ppermute(total, "seq", pairs))

    def third(self, order):
        bases = order.tied(*self.bases)
        if len(self.bases) == 1:
            bases = (bases,)
        base = sum(bases[1:], bases[0])
        self.outs = combine(self.inner, base, self.blocks)
        order.mark(self.outs[0])
        for mask in range(1, self.group):
            self.outs[mask] = exchange(self.outs[mask], "seq", mask)

    def result(self, order):
        self.outs[1:] = order.tied(*self.outs[1:])
        return self.outs


def both_exchange(array, masks):
    total = lax.axis_size("seq") * lax.axis_size("dp")
    return lax.ppermute(array, AXES, [(i, i ^ masks[i % 2]) for i in range(total)])


def turn_kernel(me_ref, x_ref, own_ref, other_ref, turned_ref):
    chips, rows, t = own_ref.shape
    core, chip = me_ref[0] % 2, me_ref[0] // 2
    span = 128 // (2 * rows)
    for block in range(chips // span):
        turned_ref[block] = jnp.transpose(x_ref[:, block * 128 : (block + 1) * 128])
    for block in range(chips // span):
        for i in range(span):
            slot = (block * span + i) ^ chip
            mine = pl.multiple_of((2 * i + core) * rows, rows)
            theirs = pl.multiple_of((2 * i + 1 - core) * rows, rows)
            own_ref[slot] = turned_ref[block, pl.ds(mine, rows)]
            other_ref[slot] = turned_ref[block, pl.ds(theirs, rows)].astype(F32)


def turn(me, x, chips):
    t, d = x.shape
    rows = d // (2 * chips)
    return in_vmem(
        turn_kernel, [me], [x], [shape((chips, rows, t), BF16), shape((chips, rows, t), F32)],
        [pltpu.VMEM((d // 128, 128, t), BF16)], cost(0, 12 * t * d), "turn_inputs",
    )


def merge_kernel(own_ref, other_ref, out_ref):
    half = own_ref.shape[-1]
    out_ref[:, :, :half] = own_ref[...]
    out_ref[:, :, half:] = other_ref[...].astype(BF16)


def merge(own, other):
    chips, rows, t = own.shape
    outs = [shape((chips, rows, 2 * t), BF16)]
    return in_vmem(merge_kernel, [], [own, other], outs, [], cost(0, 10 * own.size), "merge_inputs")[0]


def product_kernel(parts, me_ref, x_ref, own_ref, *rest):
    other_refs, out_refs = rest[: -len(parts)], rest[-len(parts) :]
    core = me_ref[0] % 2
    other = jnp.concatenate([ref[...].astype(BF16) for ref in other_refs], axis=1)
    for out_ref, (slots, start, stop) in zip(out_refs, parts):
        grads = jnp.concatenate([own_ref[:, start:stop], other[:, start:stop]], axis=0)
        rows = jnp.concatenate([x_ref[a ^ (core * (a ^ b))] for a, b in slots], axis=0)
        out_ref[...] = mm(rows, grads)


def products(me, x, own, others, parts, name):
    rows = x.shape[1]
    outs = [shape((len(slots) * rows, stop - start), F32) for slots, start, stop in parts]
    kernel = functools.partial(product_kernel, parts)
    return in_vmem(kernel, [me], [x, own, *others], outs, [], cost(0, 0), name)


class Chunk:
    def __init__(self, start, stop, orders, masks):
        self.start, self.stop = start, stop
        self.orders = [[masks[axis] for axis in order] for order in orders]
        self.step = 0

    def slots(self, sent):
        out = []
        for masks in self.orders:
            mine = []
            for pick in range(1 << (len(masks) - 1)):
                slot = masks[0] >> 1 if sent else 0
                for place, mask in enumerate(masks[1:]):
                    if pick >> (len(masks) - 2 - place) & 1:
                        slot ^= mask >> 1
                mine.append(slot)
            out.append(mine)
        return tuple(zip(*out))

    def masks(self, step):
        return [masks[step] for masks in self.orders]

    def launch(self, sending):
        self.got = both_exchange(sending, self.masks(self.step))
        self.step += 1

    def advance(self, order, small=None):
        rest, got = self.rest, order.tied(self.got)
        extra = got.shape[0] - rest.shape[0]
        if self.step == len(self.orders[0]):
            self.rest = None
            if extra:
                self.out, small = add_last(rest, got, small)
                order.mark(small)
                return small
            self.out = rest + got
            order.mark(got)
            return None
        half = rest.shape[0] // 2
        if small is None:
            sending = add_rows(rest, got, half, half)
        else:
            sending, small = add_rows_with(rest, got, small)
        order.mark(sending)
        self.launch(sending)
        self.rest = add_rows(rest, order.tied(got), 0, half)
        order.mark(self.rest)
        return small


def add_kernel(start, a_ref, b_ref, out_ref):
    rows = slice(start, start + out_ref.shape[0])
    out_ref[...] = a_ref[rows] + b_ref[rows]


def add_rows(a, b, start, rows):
    outs = [shape((rows, a.shape[1]), F32)]
    kernel = functools.partial(add_kernel, start)
    return in_vmem(kernel, [], [a, b], outs, [], cost(0, 0), "add_rows")[0]


def add_with_kernel(rest_ref, got_ref, small_ref, sending_ref, sum_ref):
    full = rest_ref.shape[0]
    half = full // 2
    total = small_ref[...]
    if got_ref.shape[0] > full:
        total = total + got_ref[full:]
    sum_ref[...] = total
    sending_ref[half:] = total
    sending_ref[:half] = rest_ref[half:] + got_ref[half:full]


def add_rows_with(rest, got, small):
    outs = [shape((rows, rest.shape[1]), F32) for rows in (rest.shape[0] // 2 + small.shape[0], small.shape[0])]
    return in_vmem(add_with_kernel, [], [rest, got, small], outs, [], cost(0, 0), "add_rows_with")


def add_last_kernel(rest_ref, got_ref, small_ref, out_ref, sum_ref):
    full = rest_ref.shape[0]
    out_ref[...] = rest_ref[...] + got_ref[:full]
    sum_ref[...] = small_ref[...] + got_ref[full:]


def add_last(rest, got, small):
    outs = [shape(rest.shape, F32), shape(small.shape, F32)]
    return in_vmem(add_last_kernel, [], [rest, got, small], outs, [], cost(0, 0), "add_last")


def first_input_kernel(grad_ref, w_ref, out_ref):
    out_ref[...] = mm_nt(grad_ref[...], w_ref[...])


def rest_input_kernel(first_ref, codes_ref, grad_a, grad_b, wa_ref, wb_ref, out_ref, term_ref):
    total = first_ref[...] + mm_nt(grad_a[...], wa_ref[...]) + mm_nt(grad_b[...], wb_ref[...])
    out_ref[...] = total.astype(BF16)
    term_ref[...] = jnp.dot(
        codes_ref[...], total, precision=lax.Precision.HIGHEST, preferred_element_type=F32
    )


def row_blocks(w):
    return pl.BlockSpec((WIDE, w.shape[1]), lambda i: (i, 0))


def out_columns(rows):
    return pl.BlockSpec((rows, WIDE), lambda i: (0, i))


def first_input_gradient(grad, w):
    t, d = grad.shape[0], w.shape[0]
    return pl.pallas_call(
        first_input_kernel,
        grid=(d // WIDE,),
        in_specs=[VMEM, row_blocks(w)],
        out_specs=out_columns(t),
        out_shape=shape((t, d), F32),
        compiler_params=params(4 * t * WIDE * 4 + 4 * WIDE * w.shape[1] + 2 * grad.size),
        cost_estimate=cost(0, 0),
        name="input_gradient_q",
    )(grad, w)


def rest_input_gradient(first, codes, grad_a, grad_b, wa, wb):
    t, d = first.shape
    rows = codes.shape[0]
    size = 8 * t * WIDE * 4 + 8 * WIDE * wa.shape[1] + 4 * grad_a.size
    return pl.pallas_call(
        rest_input_kernel,
        grid=(d // WIDE,),
        in_specs=[out_columns(t), VMEM, VMEM, VMEM, row_blocks(wa), row_blocks(wb)],
        out_specs=[out_columns(t), out_columns(rows)],
        out_shape=[shape((t, d), BF16), shape((rows, d), F32)],
        compiler_params=params(size),
        cost_estimate=cost(0, 0),
        name="input_gradient_kv",
    )(first, codes, grad_a, grad_b, wa, wb)


def body(resid, token_ids, code_proj, w_query, w_key, w_value, gain, out_grad):
    positions, width = resid.shape[1:]
    features = w_query.shape[1]
    n_dp = lax.axis_size("dp")
    total = lax.axis_size("seq") * n_dp
    me = (lax.axis_index("seq") * n_dp + lax.axis_index("dp")).astype(jnp.int32).reshape(1)
    order = Order()

    before, after = Entering(False), Entering(True)
    slots = jnp.stack([before.slot, after.slot])
    before.inner, after.inner = before.inner.reshape(1), after.inner.reshape(1)
    slots, me, before.inner, after.inner = lax.optimization_barrier((slots, me, before.inner, after.inner))
    x, code_values, keys, key_slope, values, part_kv, *pieces = embed_keys_values(
        slots, resid[0], token_ids, code_proj, w_key, w_value, before.group
    )
    before.first(pieces)
    queries, query_slope, within = queries_scores(x, w_query, keys, values)
    order.mark(within)
    before.second(order)
    own_rows, other_rows = turn(me, order.tied(x), total // 2)
    order.mark(own_rows)
    other_rows = both_exchange(other_rows, (1, 1))
    before.third(order)
    prefixes = before.result(order)

    d_att, gain_term, part_grad, *pieces = norm_gradient(
        slots, within, queries, prefixes, part_kv, out_grad[0], gain.reshape(1, features)
    )
    order.mark(d_att)
    after.first(pieces)
    grad_q, *wide_q = query_gradient(slots, order.tied(d_att), values, keys, prefixes, part_kv, query_slope)
    order.mark(grad_q)
    wide_q = [both_exchange(share, (1, 1)) for share in wide_q]
    merged = merge(own_rows, order.tied(other_rows))
    order.mark(merged)
    after.second(order)

    bits = total.bit_length() - 1
    masks = [1 << b for b in range(1, bits)]
    masks[-1] |= masks[-2]
    dims = len(masks)

    unit = features // 8
    extra = tuple(range(4, dims))

    def chunks_of(plan):
        out, start = [], 0
        for units, *orders in plan:
            axes = [tuple("xyzw".index(name) for name in order) + extra for order in orders]
            out.append(Chunk(start * unit, (start + units) * unit, axes, masks))
            start += units
        return out

    chunks_q = chunks_of([(8, "xzwy", "zxyw")])
    chunks_k = chunks_of([(8, "xzwy", "yxzw")])
    chunks_v = chunks_of([(8, "zyxw", "yxzw")])
    every = chunks_q + chunks_k + chunks_v

    def begin(chunks, own, others, name):
        own, *others = order.tied(own, *others)
        sent = products(me, merged, own, others, [(c.slots(True), c.start, c.stop) for c in chunks], name)
        order.mark(sent[0])
        for chunk, array in zip(chunks, sent):
            chunk.launch(array)
        kept = products(me, merged, order.tied(own), others, [(c.slots(False), c.start, c.stop) for c in chunks], name + "_kept")
        order.mark(kept[0])
        for chunk, array in zip(chunks, kept):
            chunk.rest = array

    begin(chunks_q, grad_q, wide_q, "weight_q")
    dk, dv = within_block(order.tied(d_att), values, keys, queries)
    order.mark(dk)
    after.third(order)
    input_grad = first_input_gradient(order.tied(grad_q), w_query)
    order.mark(input_grad)
    suffixes = after.result(order)
    outs = key_value_gradients(slots, dk, dv, values, keys, suffixes, part_grad, key_slope)
    (grad_k, *wide_k), (grad_v, *wide_v) = outs[: 1 + SHARES], outs[1 + SHARES :]
    order.mark(grad_k)
    wide_k = [both_exchange(share, (1, 1)) for share in wide_k]
    wide_v = [both_exchange(share, (1, 1)) for share in wide_v]
    begin(chunks_k, grad_k, wide_k, "weight_k")
    begin(chunks_v, grad_v, wide_v, "weight_v")
    resid_grad, code_term = rest_input_gradient(
        input_grad, code_values, order.tied(grad_k), grad_v, w_key, w_value
    )
    order.mark(code_term)
    grad_scale = 1.0 / math.sqrt(positions * total)
    codes = len(fsq_levels)
    carrier = chunks_q[0]
    edge = carrier.stop - carrier.start
    small = jnp.concatenate([gain_term.reshape(-1), code_term[:codes].reshape(-1)])
    used = small.shape[0]
    small = jnp.pad(small, (0, -used % (8 * edge))).reshape(-1, edge)

    def advance(index):
        nonlocal small
        if every[index] is carrier:
            small = carrier.advance(order, small)
        else:
            every[index].advance(order)

    small = small + order.tied(both_exchange(small, (1, 1)))
    order.mark(small)
    for index in (0, 1, 0, 2, 1, 0, 2, 1, 2):
        advance(index)
    while any(c.step < dims for c in every):
        for index in (0, 1, 2):
            if every[index].step < dims:
                advance(index)
    advance(0)
    small = small + order.tied(both_exchange(small, carrier.masks(0)))
    order.mark(small)
    for index in (1, 2):
        advance(index)
    small = small.reshape(-1)[:used] * grad_scale
    gain_sum, code_sum = small[:features], small[features:].reshape(codes, width)

    def joined(chunks):
        return jnp.concatenate([c.out for c in chunks], axis=-1)

    weights = jnp.stack([joined(chunks_q), joined(chunks_k), joined(chunks_v)], axis=1) * grad_scale
    return resid_grad[None], weights, gain_sum, code_sum


def solution(mesh):
    return jax.shard_map(
        body,
        mesh=mesh,
        in_specs=(
            P("dp", "seq", None),
            P("dp", "seq"),
            P(),
            P(),
            P(),
            P(),
            P(),
            P("dp", "seq", None),
        ),
        out_specs=(P("dp", "seq", None), P(AXES, None, None), P(), P()),
        check_vma=False,
    )
```

```python
import functools
import math

import jax
import jax.numpy as jnp
from jax import lax
from jax.experimental import pallas as pl
from jax.experimental.pallas import tpu as pltpu
from jax.sharding import PartitionSpec as P

HEADS = 8
DH = 128
PAIR = 2
WIDE = PAIR * DH
PARTS = 2
SHARES = 2
AXES = ("seq", "dp")
F32 = jnp.float32
BF16 = jnp.bfloat16
MIB = 1024 * 1024
EMBED_MIB = 41

fsq_levels = (8, 8, 8, 5, 5, 5)
fsq_bases = (1, 8, 64, 512, 2560, 12800)

NT = (((1,), (1,)), ((), ()))
TN = (((0,), (0,)), ((), ()))
VMEM = pl.BlockSpec(memory_space=pltpu.VMEM)
SMEM = pl.BlockSpec(memory_space=pltpu.SMEM)
HBM = pl.BlockSpec(memory_space=pltpu.HBM)


def mm(a, b):
    return jnp.dot(a, b, preferred_element_type=F32)


def mm_nt(a, b):
    return lax.dot_general(a, b, NT, preferred_element_type=F32)


def mm_tn(a, b):
    return lax.dot_general(a, b, TN, preferred_element_type=F32)


def params(size):
    return pltpu.CompilerParams(vmem_limit_bytes=int(size) + 5 * MIB)


def cost(flops, moved):
    return pl.CostEstimate(flops=1, bytes_accessed=1, transcendentals=0)


def shape(dims, dtype):
    return jax.ShapeDtypeStruct(dims, dtype)


def silu_and_slope(value):
    sigma = 1.0 / (1.0 + jnp.exp(-value))
    return value * sigma, sigma * (1.0 + value * (1.0 - sigma))


def head(h):
    return slice(h * DH, (h + 1) * DH)


def part_rows(t, p):
    return slice(p * (t // PARTS), (p + 1) * (t // PARTS))


def hand_out(slot, part_sums, pieces):
    share = pieces[0].shape[0]
    for mask, piece in enumerate(pieces):
        heads = pl.ds((slot ^ mask) * share, share)
        total = part_sums[0, heads]
        for p in range(1, PARTS):
            total = total + part_sums[p, heads]
        piece[...] = total


def take_in(slot, pieces, out_ref):
    share = pieces[0].shape[0]
    for mask, piece in enumerate(pieces):
        out_ref[pl.ds((slot ^ mask) * share, share)] = piece[...]


def in_vmem(kernel, slots, inputs, outs, scratch, price, name):
    size = sum(math.prod(a.shape) * a.dtype.itemsize for a in [*inputs, *outs, *scratch])
    return pl.pallas_call(
        kernel,
        in_specs=[SMEM] * len(slots) + [VMEM] * len(inputs),
        out_specs=[VMEM] * len(outs),
        out_shape=outs,
        scratch_shapes=scratch,
        compiler_params=params(size),
        cost_estimate=price,
        name=name,
    )(*slots, *inputs)


def embed_kernel(
    slots, packed_ref, resid_hbm, wk_hbm, wv_hbm,
    x_ref, codes_ref, k_ref, slope_ref, v_ref, kv_ref, *rest,
):
    pieces = rest[:-4]
    resid_ref, wk_ref, wv_ref, sems = rest[-4:]
    t, d = x_ref.shape
    hd = k_ref.shape[1]
    half = hd // 2
    moves = [(resid_hbm, resid_ref)]
    for hbm, ref in ((wk_hbm, wk_ref), (wv_hbm, wv_ref)):
        for r in range(2):
            at = pl.ds(r * (d // 2), d // 2)
            moves.append((hbm.at[at], ref.at[at]))
    incoming = [pltpu.make_async_copy(hbm, ref, sems.at[i]) for i, (hbm, ref) in enumerate(moves)]
    for copy in incoming:
        copy.start()
    count = len(fsq_levels)
    ids = packed_ref[count : count + 1, :t].astype(jnp.int32)
    code_list = []
    for fsq_level, fsq_base in zip(fsq_levels, fsq_bases):
        digit = lax.rem(lax.div(ids, fsq_base), fsq_level)
        code_list.append((2.0 * digit.astype(F32) - (fsq_level - 1)) / (fsq_level - 1))
    for _ in range(codes_ref.shape[0] - count):
        code_list.append(jnp.zeros_like(code_list[0]))
    codes = jnp.concatenate(code_list, axis=0)
    codes_ref[...] = codes
    turned = jnp.transpose(codes)
    incoming[0].wait()
    step = 64
    for r in range(0, t, step):
        summed = resid_ref[r : r + step].astype(F32)
        for index in range(count):
            summed = summed + turned[r : r + step, index : index + 1] * packed_ref[index : index + 1]
        x_ref[r : r + step] = summed.astype(BF16)
    x = x_ref[...]
    incoming[1].wait()
    incoming[2].wait()
    for c in range(2):
        at = slice(c * half, (c + 1) * half)
        key, slope = silu_and_slope(mm(x, wk_ref[:, at]))
        k_ref[:, at] = key.astype(BF16)
        slope_ref[:, at] = slope
    incoming[3].wait()
    incoming[4].wait()
    for c in range(2):
        at = slice(c * half, (c + 1) * half)
        value = mm(x, wv_ref[:, at]).astype(BF16)
        v_ref[:, at] = value
        for h in range(half // DH):
            which = c * (half // DH) + h
            for p in range(PARTS):
                rows = part_rows(t, p)
                kv_ref[p, which] = mm_tn(k_ref[rows, head(which)], value[rows, head(h)])
    hand_out(slots[0], kv_ref, pieces)


def embed_keys_values(slots, resid, token_ids, code_proj, w_key, w_value, group):
    t, d = resid.shape
    hd = w_key.shape[1]
    heads = hd // DH
    ids = jnp.pad(token_ids.astype(F32), ((0, 0), (0, d - t)))
    packed = jnp.concatenate([code_proj, ids], axis=0)
    return pl.pallas_call(
        embed_kernel,
        in_specs=[SMEM, VMEM] + [HBM] * 3,
        out_specs=[VMEM] * (6 + group),
        out_shape=[
            shape((t, d), BF16),
            shape((8, t), F32),
            shape((t, hd), BF16),
            shape((t, hd), F32),
            shape((t, hd), BF16),
            shape((PARTS, heads, DH, DH), F32),
        ]
        + [shape((heads // group, DH, DH), F32)] * group,
        scratch_shapes=[
            pltpu.VMEM((t, d), BF16),
            pltpu.VMEM((d, hd), BF16),
            pltpu.VMEM((d, hd), BF16),
            pltpu.SemaphoreType.DMA((5,)),
        ],
        compiler_params=params(EMBED_MIB * MIB),
        cost_estimate=cost(4 * t * d * hd, 4 * d * hd + 10 * t * hd),
        name="embed_keys_values",
    )(slots, packed, resid, w_key, w_value)


def causal_mask(t, transposed):
    rows = lax.broadcasted_iota(jnp.int32, (t, t), 0)
    cols = lax.broadcasted_iota(jnp.int32, (t, t), 1)
    return rows <= cols if transposed else cols <= rows


def masked(mask, product):
    return jnp.where(mask, product, 0.0).astype(BF16)


def query_kernel(x_ref, wq_ref, k_ref, v_ref, q_ref, slope_ref, sv_ref):
    t = x_ref.shape[0]
    hd = q_ref.shape[1]
    half = hd // 2
    mask = causal_mask(t // PARTS, False)
    for c in range(2):
        at = slice(c * half, (c + 1) * half)
        query, slope = silu_and_slope(mm(x_ref[...], wq_ref[:, at]))
        query = query.astype(BF16)
        q_ref[:, at] = query
        slope_ref[:, at] = slope
        for h in range(half // DH):
            at = head(c * (half // DH) + h)
            for p in range(PARTS):
                rows = part_rows(t, p)
                scores = masked(mask, mm_nt(query[rows, head(h)], k_ref[rows, at]))
                sv_ref[rows, at] = mm(scores, v_ref[rows, at])


def queries_scores(x, w_query, keys, values):
    t, d = x.shape
    hd = w_query.shape[1]
    outs = [shape((t, hd), BF16), shape((t, hd), F32), shape((t, hd), F32)]
    price = cost(2 * t * d * hd + 2 * t * t * hd, 2 * d * hd + 14 * t * hd)
    return in_vmem(query_kernel, [], [x, w_query, keys, values], outs, [], price, "queries_scores")


def norm_kernel(slots, sv_ref, q_ref, kv_ref, og_ref, gain_ref, *rest):
    group = (len(rest) - 4) // 2
    prefixes, (datt_ref, term_ref, grad_ref), outs = rest[:group], rest[group : group + 3], rest[group + 3 : -1]
    state_ref = rest[-1]
    take_in(slots[0], prefixes, state_ref)
    t, hd = q_ref.shape
    for h in range(hd // DH):
        at = head(h)
        term = None
        state = state_ref[h]
        for p in range(PARTS):
            rows = part_rows(t, p)
            if p:
                state = state + kv_ref[p - 1, h]
            query = q_ref[rows, at]
            attended = sv_ref[rows, at] + mm(query, state.astype(BF16))
            inverse = lax.rsqrt(jnp.mean(attended * attended, axis=-1, keepdims=True) + 1e-06)
            normed = attended * inverse
            grad = og_ref[rows, at].astype(F32)
            more = jnp.sum(grad * normed, axis=0, keepdims=True)
            term = more if term is None else term + more
            d_normed = grad * gain_ref[:, at]
            inner = jnp.mean(d_normed * normed, axis=-1, keepdims=True)
            d_att = ((d_normed - normed * inner) * inverse).astype(BF16)
            datt_ref[rows, at] = d_att
            grad_ref[p, h] = mm_tn(query, d_att)
        term_ref[:, at] = term
    hand_out(slots[1], grad_ref, outs)


def norm_gradient(slots, sv, queries, prefixes, part_kv, out_grad, gain):
    t, hd = sv.shape
    heads = hd // DH
    group = len(prefixes)
    outs = [shape((t, hd), BF16), shape((1, hd), F32), shape((PARTS, heads, DH, DH), F32)]
    outs += [shape((heads // group, DH, DH), F32)] * group
    return in_vmem(
        norm_kernel, [slots], [sv, queries, part_kv, out_grad, gain, *prefixes], outs,
        [pltpu.VMEM((heads, DH, DH), F32)], cost(4 * t * hd * DH, 10 * t * hd), "norm_gradient",
    )


def store_wide(refs, rows, h, grad):
    width = refs[0].shape[1]
    start = h * DH % width
    refs[h * DH // width][rows, start : start + DH] = grad.astype(F32)


def dquery_kernel(slots, datt_ref, v_ref, k_ref, kv_ref, slope_ref, *rest):
    prefixes, (g16_ref, state_ref) = rest[:-2], rest[-2:]
    take_in(slots[0], prefixes, state_ref)
    t, hd = datt_ref.shape
    mask = causal_mask(t // PARTS, False)
    for h in range(hd // DH):
        at = head(h)
        state = state_ref[h]
        for p in range(PARTS):
            rows = part_rows(t, p)
            if p:
                state = state + kv_ref[p - 1, h]
            d_att = datt_ref[rows, at]
            back = masked(mask, mm_nt(d_att, v_ref[rows, at]))
            d_query = mm(back, k_ref[rows, at]) + mm_nt(d_att, state.astype(BF16))
            grad = (d_query * slope_ref[rows, at]).astype(BF16)
            g16_ref[rows, at] = grad


def query_gradient(slots, d_att, values, keys, prefixes, part_kv, slope):
    t, hd = d_att.shape
    return in_vmem(
        dquery_kernel, [slots], [d_att, values, keys, part_kv, slope, *prefixes],
        [shape((t, hd), BF16)], [pltpu.VMEM((hd // DH, DH, DH), F32)],
        cost(2 * t * t * hd, 16 * t * hd), "query_gradient",
    )[0]


def widen_kernel(grad_ref, *wide):
    width = wide[0].shape[1]
    for index, ref in enumerate(wide):
        ref[...] = grad_ref[:, index * width : (index + 1) * width].astype(F32)


def widen(grad):
    t, hd = grad.shape
    outs = [shape((t, hd // SHARES), F32)] * SHARES
    return in_vmem(widen_kernel, [], [grad], outs, [], cost(0, 0), "widen")


def within_kernel(datt_ref, v_ref, k_ref, q_ref, dk_ref, dv_ref):
    t, hd = datt_ref.shape
    mask = causal_mask(t // PARTS, True)
    for h in range(hd // DH):
        at = head(h)
        for p in range(PARTS):
            rows = part_rows(t, p)
            d_att, query = datt_ref[rows, at], q_ref[rows, at]
            back = masked(mask, mm_nt(v_ref[rows, at], d_att))
            dk_ref[rows, at] = mm(back, query)
            scores = masked(mask, mm_nt(k_ref[rows, at], query))
            dv_ref[rows, at] = mm(scores, d_att)


def within_block(d_att, values, keys, queries):
    t, hd = d_att.shape
    return in_vmem(
        within_kernel, [], [d_att, values, keys, queries], [shape((t, hd), F32)] * 2, [],
        cost(4 * t * t * hd, 16 * t * hd), "within_block",
    )


def dkv_kernel(slots, dk_ref, dv_ref, v_ref, k_ref, grad_ref, slope_ref, *rest):
    suffixes, outs, state_ref = rest[: -3 - 2 * SHARES], rest[-3 - 2 * SHARES : -1], rest[-1]
    (k16, *wide_k), (v16, *wide_v) = outs[: 1 + SHARES], outs[1 + SHARES :]
    take_in(slots[1], suffixes, state_ref)
    t, hd = dk_ref.shape
    for h in range(hd // DH):
        at = head(h)
        state = state_ref[h]
        for p in reversed(range(PARTS)):
            rows = part_rows(t, p)
            if p < PARTS - 1:
                state = state + grad_ref[p + 1, h]
            suffix = state.astype(BF16)
            d_key = dk_ref[rows, at] + mm_nt(v_ref[rows, at], suffix)
            grad = (d_key * slope_ref[rows, at]).astype(BF16)
            k16[rows, at] = grad
            store_wide(wide_k, rows, h, grad)
            grad = (dv_ref[rows, at] + mm(k_ref[rows, at], suffix)).astype(BF16)
            v16[rows, at] = grad
            store_wide(wide_v, rows, h, grad)


def key_value_gradients(slots, dk, dv, values, keys, suffixes, part_grad, slope):
    t, hd = dk.shape
    return in_vmem(
        dkv_kernel, [slots], [dk, dv, values, keys, part_grad, slope, *suffixes],
        ([shape((t, hd), BF16)] + [shape((t, hd // SHARES), F32)] * SHARES) * 2,
        [pltpu.VMEM((hd // DH, DH, DH), F32)],
        cost(4 * t * hd * DH, 28 * t * hd), "key_value_gradients",
    )


class Order:
    def __init__(self):
        self.last = None

    def tied(self, *arrays):
        if self.last is not None:
            *arrays, _ = lax.optimization_barrier((*arrays, self.last))
        return arrays[0] if len(arrays) == 1 else tuple(arrays)

    def mark(self, array):
        self.last = array


def exchange(array, axis, mask):
    count = lax.axis_size(axis)
    return lax.ppermute(array, axis, [(i, i ^ mask) for i in range(count)])


def combine_kernel(inner, base_ref, *refs):
    group = len(refs) // 2
    blocks, outs = refs[:group], refs[group:]
    for mask, out_ref in enumerate(outs):
        out_ref[...] = base_ref[...]
        for other, block in enumerate(blocks):
            if other != mask:

                @pl.when((inner[0] ^ other) < (inner[0] ^ mask))
                def _(out_ref=out_ref, block=block):
                    out_ref[...] += block[...]


def combine(inner, base, blocks):
    outs = [shape(base.shape, F32)] * len(blocks)
    return list(in_vmem(combine_kernel, [inner], [base, *blocks], outs, [], cost(0, 0), "combine"))


class Entering:
    def __init__(self, reverse):
        self.reverse = reverse
        self.count = lax.axis_size("seq")
        self.group = min(HEADS // PAIR, self.count)
        place = lax.axis_index("seq")
        if reverse:
            place = self.count - 1 - place
        self.inner, cluster = place % self.group, place // self.group
        self.twist = self.group // 2
        self.slot = (self.inner ^ (self.twist * (cluster % 2))).astype(jnp.int32)
        self.inner = self.inner.astype(jnp.int32)

    def first(self, pieces):
        self.blocks = [pieces[0]]
        for mask in range(1, self.group):
            self.blocks.append(exchange(pieces[mask], "seq", mask))

    def second(self, order):
        self.blocks[1:] = order.tied(*self.blocks[1:])
        total = sum(self.blocks[1:], self.blocks[0])
        order.mark(total)
        group, twist, count = self.group, self.twist, self.count
        clusters = count // group
        self.bases = []
        for shift in range(1, clusters):
            pairs = []
            for source in range(clusters - shift):
                for slot in range(group):
                    a = source * group + (slot ^ (twist * (source % 2)))
                    target = source + shift
                    b = target * group + (slot ^ (twist * (target % 2)))
                    pairs.append((count - 1 - a, count - 1 - b) if self.reverse else (a, b))
            self.bases.append(lax.ppermute(total, "seq", pairs))

    def third(self, order):
        bases = order.tied(*self.bases)
        if len(self.bases) == 1:
            bases = (bases,)
        base = sum(bases[1:], bases[0])
        self.outs = combine(self.inner, base, self.blocks)
        order.mark(self.outs[0])
        for mask in range(1, self.group):
            self.outs[mask] = exchange(self.outs[mask], "seq", mask)

    def result(self, order):
        self.outs[1:] = order.tied(*self.outs[1:])
        return self.outs


def both_exchange(array, masks):
    total = lax.axis_size("seq") * lax.axis_size("dp")
    return lax.ppermute(array, AXES, [(i, i ^ masks[i % 2]) for i in range(total)])


def turn_kernel(me_ref, x_ref, own_ref, other_ref, turned_ref):
    chips, rows, t = own_ref.shape
    core, chip = me_ref[0] % 2, me_ref[0] // 2
    span = 128 // (2 * rows)
    for block in range(chips // span):
        turned_ref[block] = jnp.transpose(x_ref[:, block * 128 : (block + 1) * 128])
    for block in range(chips // span):
        for i in range(span):
            slot = (block * span + i) ^ chip
            mine = pl.multiple_of((2 * i + core) * rows, rows)
            theirs = pl.multiple_of((2 * i + 1 - core) * rows, rows)
            own_ref[slot] = turned_ref[block, pl.ds(mine, rows)]
            other_ref[slot] = turned_ref[block, pl.ds(theirs, rows)].astype(F32)


def turn(me, x, chips):
    t, d = x.shape
    rows = d // (2 * chips)
    return in_vmem(
        turn_kernel, [me], [x], [shape((chips, rows, t), BF16), shape((chips, rows, t), F32)],
        [pltpu.VMEM((d // 128, 128, t), BF16)], cost(0, 12 * t * d), "turn_inputs",
    )


def merge_kernel(own_ref, other_ref, out_ref):
    half = own_ref.shape[-1]
    out_ref[:, :, :half] = own_ref[...]
    out_ref[:, :, half:] = other_ref[...].astype(BF16)


def merge(own, other):
    chips, rows, t = own.shape
    outs = [shape((chips, rows, 2 * t), BF16)]
    return in_vmem(merge_kernel, [], [own, other], outs, [], cost(0, 10 * own.size), "merge_inputs")[0]


def product_kernel(parts, me_ref, x_ref, own_ref, *rest):
    other_refs, out_refs = rest[: -len(parts)], rest[-len(parts) :]
    core = me_ref[0] % 2
    other = jnp.concatenate([ref[...].astype(BF16) for ref in other_refs], axis=1)
    for out_ref, (slots, start, stop) in zip(out_refs, parts):
        grads = jnp.concatenate([own_ref[:, start:stop], other[:, start:stop]], axis=0)
        rows = jnp.concatenate([x_ref[a ^ (core * (a ^ b))] for a, b in slots], axis=0)
        out_ref[...] = mm(rows, grads)


def products(me, x, own, others, parts, name):
    rows = x.shape[1]
    outs = [shape((len(slots) * rows, stop - start), F32) for slots, start, stop in parts]
    kernel = functools.partial(product_kernel, parts)
    return in_vmem(kernel, [me], [x, own, *others], outs, [], cost(0, 0), name)


class Chunk:
    def __init__(self, start, stop, orders, masks):
        self.start, self.stop = start, stop
        self.orders = [[masks[axis] for axis in order] for order in orders]
        self.step = 0

    def slots(self, sent):
        out = []
        for masks in self.orders:
            mine = []
            for pick in range(1 << (len(masks) - 1)):
                slot = masks[0] >> 1 if sent else 0
                for place, mask in enumerate(masks[1:]):
                    if pick >> (len(masks) - 2 - place) & 1:
                        slot ^= mask >> 1
                mine.append(slot)
            out.append(mine)
        return tuple(zip(*out))

    def masks(self, step):
        return [masks[step] for masks in self.orders]

    def launch(self, sending):
        self.got = both_exchange(sending, self.masks(self.step))
        self.step += 1

    def advance(self, order, small=None):
        rest, got = self.rest, order.tied(self.got)
        extra = got.shape[0] - rest.shape[0]
        if self.step == len(self.orders[0]):
            self.rest = None
            if extra:
                self.out, small = add_last(rest, got, small)
                order.mark(small)
                return small
            self.out = rest + got
            order.mark(got)
            return None
        half = rest.shape[0] // 2
        if small is None:
            sending = add_rows(rest, got, half, half)
        else:
            sending, small = add_rows_with(rest, got, small)
        order.mark(sending)
        self.launch(sending)
        self.rest = add_rows(rest, order.tied(got), 0, half)
        order.mark(self.rest)
        return small


def add_kernel(start, a_ref, b_ref, out_ref):
    rows = slice(start, start + out_ref.shape[0])
    out_ref[...] = a_ref[rows] + b_ref[rows]


def add_rows(a, b, start, rows):
    outs = [shape((rows, a.shape[1]), F32)]
    kernel = functools.partial(add_kernel, start)
    return in_vmem(kernel, [], [a, b], outs, [], cost(0, 0), "add_rows")[0]


def add_with_kernel(rest_ref, got_ref, small_ref, sending_ref, sum_ref):
    full = rest_ref.shape[0]
    half = full // 2
    total = small_ref[...]
    if got_ref.shape[0] > full:
        total = total + got_ref[full:]
    sum_ref[...] = total
    sending_ref[half:] = total
    sending_ref[:half] = rest_ref[half:] + got_ref[half:full]


def add_rows_with(rest, got, small):
    outs = [shape((rows, rest.shape[1]), F32) for rows in (rest.shape[0] // 2 + small.shape[0], small.shape[0])]
    return in_vmem(add_with_kernel, [], [rest, got, small], outs, [], cost(0, 0), "add_rows_with")


def add_last_kernel(rest_ref, got_ref, small_ref, out_ref, sum_ref):
    full = rest_ref.shape[0]
    out_ref[...] = rest_ref[...] + got_ref[:full]
    sum_ref[...] = small_ref[...] + got_ref[full:]


def add_last(rest, got, small):
    outs = [shape(rest.shape, F32), shape(small.shape, F32)]
    return in_vmem(add_last_kernel, [], [rest, got, small], outs, [], cost(0, 0), "add_last")


def first_input_kernel(grad_ref, w_ref, out_ref):
    out_ref[...] = mm_nt(grad_ref[...], w_ref[...])


def rest_input_kernel(first_ref, codes_ref, grad_a, grad_b, wa_ref, wb_ref, out_ref, term_ref):
    total = first_ref[...] + mm_nt(grad_a[...], wa_ref[...]) + mm_nt(grad_b[...], wb_ref[...])
    out_ref[...] = total.astype(BF16)
    term_ref[...] = jnp.dot(
        codes_ref[...], total, precision=lax.Precision.HIGHEST, preferred_element_type=F32
    )


def row_blocks(w):
    return pl.BlockSpec((WIDE, w.shape[1]), lambda i: (i, 0))


def out_columns(rows):
    return pl.BlockSpec((rows, WIDE), lambda i: (0, i))


def first_input_gradient(grad, w):
    t, d = grad.shape[0], w.shape[0]
    return pl.pallas_call(
        first_input_kernel,
        grid=(d // WIDE,),
        in_specs=[VMEM, row_blocks(w)],
        out_specs=out_columns(t),
        out_shape=shape((t, d), F32),
        compiler_params=params(4 * t * WIDE * 4 + 4 * WIDE * w.shape[1] + 2 * grad.size),
        cost_estimate=cost(0, 0),
        name="input_gradient_q",
    )(grad, w)


def rest_input_gradient(first, codes, grad_a, grad_b, wa, wb):
    t, d = first.shape
    rows = codes.shape[0]
    size = 8 * t * WIDE * 4 + 8 * WIDE * wa.shape[1] + 4 * grad_a.size
    return pl.pallas_call(
        rest_input_kernel,
        grid=(d // WIDE,),
        in_specs=[out_columns(t), VMEM, VMEM, VMEM, row_blocks(wa), row_blocks(wb)],
        out_specs=[out_columns(t), out_columns(rows)],
        out_shape=[shape((t, d), BF16), shape((rows, d), F32)],
        compiler_params=params(size),
        cost_estimate=cost(0, 0),
        name="input_gradient_kv",
    )(first, codes, grad_a, grad_b, wa, wb)


def body(resid, token_ids, code_proj, w_query, w_key, w_value, gain, out_grad):
    positions, width = resid.shape[1:]
    features = w_query.shape[1]
    n_dp = lax.axis_size("dp")
    total = lax.axis_size("seq") * n_dp
    me = (lax.axis_index("seq") * n_dp + lax.axis_index("dp")).astype(jnp.int32).reshape(1)
    order = Order()

    before, after = Entering(False), Entering(True)
    slots = jnp.stack([before.slot, after.slot])
    before.inner, after.inner = before.inner.reshape(1), after.inner.reshape(1)
    slots, me, before.inner, after.inner = lax.optimization_barrier((slots, me, before.inner, after.inner))
    x, code_values, keys, key_slope, values, part_kv, *pieces = embed_keys_values(
        slots, resid[0], token_ids, code_proj, w_key, w_value, before.group
    )
    before.first(pieces)
    queries, query_slope, within = queries_scores(x, w_query, keys, values)
    order.mark(within)
    own_rows, other_rows = turn(me, order.tied(x), total // 2)
    order.mark(own_rows)
    before.second(order)
    other_rows = both_exchange(order.tied(other_rows), (1, 1))
    before.third(order)
    prefixes = before.result(order)

    d_att, gain_term, part_grad, *pieces = norm_gradient(
        slots, within, queries, prefixes, part_kv, out_grad[0], gain.reshape(1, features)
    )
    order.mark(d_att)
    after.first(pieces)
    grad_q = query_gradient(slots, order.tied(d_att), values, keys, prefixes, part_kv, query_slope)
    order.mark(grad_q)
    merged = merge(own_rows, order.tied(other_rows))
    order.mark(merged)
    after.second(order)
    wide_q = widen(order.tied(grad_q))
    order.mark(wide_q[0])
    wide_q = [both_exchange(share, (1, 1)) for share in wide_q]
    dk, dv = within_block(order.tied(d_att), values, keys, queries)
    order.mark(dk)

    bits = total.bit_length() - 1
    masks = [1 << b for b in range(1, bits)]
    masks[-1] |= masks[-2]
    dims = len(masks)

    unit = features // 8
    extra = tuple(range(4, dims))

    def chunks_of(plan):
        out, start = [], 0
        for units, *orders in plan:
            axes = [tuple("xyzw".index(name) for name in order) + extra for order in orders]
            out.append(Chunk(start * unit, (start + units) * unit, axes, masks))
            start += units
        return out

    chunks_q = chunks_of([(8, "xzwy", "zxyw")])
    chunks_k = chunks_of([(8, "xzwy", "yxzw")])
    chunks_v = chunks_of([(8, "zyxw", "yxzw")])
    every = chunks_q + chunks_k + chunks_v

    def begin(chunks, own, others, name):
        own, *others = order.tied(own, *others)
        sent = products(me, merged, own, others, [(c.slots(True), c.start, c.stop) for c in chunks], name)
        order.mark(sent[0])
        for chunk, array in zip(chunks, sent):
            chunk.launch(array)
        kept = products(me, merged, order.tied(own), others, [(c.slots(False), c.start, c.stop) for c in chunks], name + "_kept")
        order.mark(kept[0])
        for chunk, array in zip(chunks, kept):
            chunk.rest = array

    begin(chunks_q, grad_q, wide_q, "weight_q")
    after.third(order)
    input_grad = first_input_gradient(order.tied(grad_q), w_query)
    order.mark(input_grad)
    suffixes = after.result(order)
    outs = key_value_gradients(slots, dk, dv, values, keys, suffixes, part_grad, key_slope)
    (grad_k, *wide_k), (grad_v, *wide_v) = outs[: 1 + SHARES], outs[1 + SHARES :]
    order.mark(grad_k)
    wide_k = [both_exchange(share, (1, 1)) for share in wide_k]
    wide_v = [both_exchange(share, (1, 1)) for share in wide_v]
    begin(chunks_k, grad_k, wide_k, "weight_k")
    begin(chunks_v, grad_v, wide_v, "weight_v")
    resid_grad, code_term = rest_input_gradient(
        input_grad, code_values, order.tied(grad_k), grad_v, w_key, w_value
    )
    order.mark(code_term)
    grad_scale = 1.0 / math.sqrt(positions * total)
    codes = len(fsq_levels)
    carrier = chunks_q[0]
    edge = carrier.stop - carrier.start
    small = jnp.concatenate([gain_term.reshape(-1), code_term[:codes].reshape(-1)])
    used = small.shape[0]
    small = jnp.pad(small, (0, -used % (8 * edge))).reshape(-1, edge)

    def advance(index):
        nonlocal small
        if every[index] is carrier:
            small = carrier.advance(order, small)
        else:
            every[index].advance(order)

    small = small + order.tied(both_exchange(small, (1, 1)))
    order.mark(small)
    for index in (0, 1, 0, 2, 1, 0, 2, 1, 2):
        advance(index)
    while any(c.step < dims for c in every):
        for index in (0, 1, 2):
            if every[index].step < dims:
                advance(index)
    advance(0)
    small = small + order.tied(both_exchange(small, carrier.masks(0)))
    order.mark(small)
    for index in (1, 2):
        advance(index)
    small = small.reshape(-1)[:used] * grad_scale
    gain_sum, code_sum = small[:features], small[features:].reshape(codes, width)

    def joined(chunks):
        return jnp.concatenate([c.out for c in chunks], axis=-1)

    weights = jnp.stack([joined(chunks_q), joined(chunks_k), joined(chunks_v)], axis=1) * grad_scale
    return resid_grad[None], weights, gain_sum, code_sum


def solution(mesh):
    return jax.shard_map(
        body,
        mesh=mesh,
        in_specs=(
            P("dp", "seq", None),
            P("dp", "seq"),
            P(),
            P(),
            P(),
            P(),
            P(),
            P("dp", "seq", None),
        ),
        out_specs=(P("dp", "seq", None), P(AXES, None, None), P(), P()),
        check_vma=False,
    )
```

```python
import functools
import math

import jax
import jax.numpy as jnp
from jax import lax
from jax.experimental import pallas as pl
from jax.experimental.pallas import tpu as pltpu
from jax.sharding import PartitionSpec as P

HEADS = 8
DH = 128
PAIR = 2
WIDE = PAIR * DH
PARTS = 2
SHARES = 2
AXES = ("seq", "dp")
F32 = jnp.float32
BF16 = jnp.bfloat16
MIB = 1024 * 1024
EMBED_MIB = 43

fsq_levels = (8, 8, 8, 5, 5, 5)
fsq_bases = (1, 8, 64, 512, 2560, 12800)

NT = (((1,), (1,)), ((), ()))
TN = (((0,), (0,)), ((), ()))
VMEM = pl.BlockSpec(memory_space=pltpu.VMEM)
SMEM = pl.BlockSpec(memory_space=pltpu.SMEM)
HBM = pl.BlockSpec(memory_space=pltpu.HBM)


def mm(a, b):
    return jnp.dot(a, b, preferred_element_type=F32)


def mm_nt(a, b):
    return lax.dot_general(a, b, NT, preferred_element_type=F32)


def mm_tn(a, b):
    return lax.dot_general(a, b, TN, preferred_element_type=F32)


def params(size):
    return pltpu.CompilerParams(vmem_limit_bytes=int(size) + 3 * MIB)


def cost(flops, moved):
    return pl.CostEstimate(flops=1, bytes_accessed=1, transcendentals=0)


def shape(dims, dtype):
    return jax.ShapeDtypeStruct(dims, dtype)


def silu_and_slope(value):
    sigma = 1.0 / (1.0 + jnp.exp(-value))
    return value * sigma, sigma * (1.0 + value * (1.0 - sigma))


def head(h):
    return slice(h * DH, (h + 1) * DH)


def part_rows(t, p):
    return slice(p * (t // PARTS), (p + 1) * (t // PARTS))


def hand_out(slot, part_sums, pieces):
    share = pieces[0].shape[0]
    for mask, piece in enumerate(pieces):
        heads = pl.ds((slot ^ mask) * share, share)
        total = part_sums[0, heads]
        for p in range(1, PARTS):
            total = total + part_sums[p, heads]
        piece[...] = total


def take_in(slot, pieces, out_ref):
    share = pieces[0].shape[0]
    for mask, piece in enumerate(pieces):
        out_ref[pl.ds((slot ^ mask) * share, share)] = piece[...]


def in_vmem(kernel, slots, inputs, outs, scratch, price, name):
    size = sum(math.prod(a.shape) * a.dtype.itemsize for a in [*inputs, *outs, *scratch])
    return pl.pallas_call(
        kernel,
        in_specs=[SMEM] * len(slots) + [VMEM] * len(inputs),
        out_specs=[VMEM] * len(outs),
        out_shape=outs,
        scratch_shapes=scratch,
        compiler_params=params(size),
        cost_estimate=price,
        name=name,
    )(*slots, *inputs)


def embed_kernel(
    slots, packed_ref, resid_hbm, wk_hbm, wv_hbm,
    x_ref, codes_ref, k_ref, slope_ref, v_ref, kv_ref, *rest,
):
    pieces = rest[:-4]
    resid_ref, wk_ref, wv_ref, sems = rest[-4:]
    t, d = x_ref.shape
    hd = k_ref.shape[1]
    half = hd // 2
    moves = [(resid_hbm, resid_ref)]
    for hbm, ref in ((wk_hbm, wk_ref), (wv_hbm, wv_ref)):
        for r in range(2):
            at = pl.ds(r * (d // 2), d // 2)
            moves.append((hbm.at[at], ref.at[at]))
    incoming = [pltpu.make_async_copy(hbm, ref, sems.at[i]) for i, (hbm, ref) in enumerate(moves)]
    for copy in incoming:
        copy.start()
    count = len(fsq_levels)
    ids = packed_ref[count : count + 1, :t].astype(jnp.int32)
    code_list = []
    for fsq_level, fsq_base in zip(fsq_levels, fsq_bases):
        digit = lax.rem(lax.div(ids, fsq_base), fsq_level)
        code_list.append((2.0 * digit.astype(F32) - (fsq_level - 1)) / (fsq_level - 1))
    for _ in range(codes_ref.shape[0] - count):
        code_list.append(jnp.zeros_like(code_list[0]))
    codes = jnp.concatenate(code_list, axis=0)
    codes_ref[...] = codes
    turned = jnp.transpose(codes)
    incoming[0].wait()
    step = 64
    for p in range(PARTS):
        rows = part_rows(t, p)
        for r in range(rows.start, rows.stop, step):
            summed = resid_ref[r : r + step].astype(F32)
            for index in range(count):
                summed = summed + turned[r : r + step, index : index + 1] * packed_ref[index : index + 1]
            x_ref[r : r + step] = summed.astype(BF16)
        if p == 0:
            incoming[1].wait()
            incoming[2].wait()
        for c in range(2):
            at = slice(c * half, (c + 1) * half)
            key, slope = silu_and_slope(mm(x_ref[rows], wk_ref[:, at]))
            k_ref[rows, at] = key.astype(BF16)
            slope_ref[rows, at] = slope
    x = x_ref[...]
    incoming[3].wait()
    incoming[4].wait()
    for c in range(2):
        at = slice(c * half, (c + 1) * half)
        value = mm(x, wv_ref[:, at]).astype(BF16)
        v_ref[:, at] = value
        for h in range(half // DH):
            which = c * (half // DH) + h
            for p in range(PARTS):
                rows = part_rows(t, p)
                kv_ref[p, which] = mm_tn(k_ref[rows, head(which)], value[rows, head(h)])
    hand_out(slots[0], kv_ref, pieces)


def embed_keys_values(slots, resid, token_ids, code_proj, w_key, w_value, group):
    t, d = resid.shape
    hd = w_key.shape[1]
    heads = hd // DH
    ids = jnp.pad(token_ids, ((0, 0), (0, d - t)))
    packed = jnp.concatenate([code_proj, ids.astype(F32)], axis=0)
    return pl.pallas_call(
        embed_kernel,
        in_specs=[SMEM, VMEM] + [HBM] * 3,
        out_specs=[VMEM] * (6 + group),
        out_shape=[
            shape((t, d), BF16),
            shape((8, t), F32),
            shape((t, hd), BF16),
            shape((t, hd), F32),
            shape((t, hd), BF16),
            shape((PARTS, heads, DH, DH), F32),
        ]
        + [shape((heads // group, DH, DH), F32)] * group,
        scratch_shapes=[
            pltpu.VMEM((t, d), BF16),
            pltpu.VMEM((d, hd), BF16),
            pltpu.VMEM((d, hd), BF16),
            pltpu.SemaphoreType.DMA((5,)),
        ],
        compiler_params=params(EMBED_MIB * MIB),
        cost_estimate=cost(4 * t * d * hd, 4 * d * hd + 10 * t * hd),
        name="embed_keys_values",
    )(slots, packed, resid, w_key, w_value)


def causal_mask(t, transposed):
    rows = lax.broadcasted_iota(jnp.int32, (t, t), 0)
    cols = lax.broadcasted_iota(jnp.int32, (t, t), 1)
    return rows <= cols if transposed else cols <= rows


def masked(mask, product):
    return jnp.where(mask, product, 0.0).astype(BF16)


def query_kernel(x_ref, wq_ref, k_ref, v_ref, q_ref, slope_ref, sv_ref):
    t = x_ref.shape[0]
    hd = q_ref.shape[1]
    half = hd // 2
    mask = causal_mask(t // PARTS, False)
    for c in range(2):
        at = slice(c * half, (c + 1) * half)
        query, slope = silu_and_slope(mm(x_ref[...], wq_ref[:, at]))
        query = query.astype(BF16)
        q_ref[:, at] = query
        slope_ref[:, at] = slope
        for h in range(half // DH):
            at = head(c * (half // DH) + h)
            for p in range(PARTS):
                rows = part_rows(t, p)
                scores = masked(mask, mm_nt(query[rows, head(h)], k_ref[rows, at]))
                sv_ref[rows, at] = mm(scores, v_ref[rows, at])


def queries_scores(x, w_query, keys, values):
    t, d = x.shape
    hd = w_query.shape[1]
    outs = [shape((t, hd), BF16), shape((t, hd), F32), shape((t, hd), F32)]
    price = cost(2 * t * d * hd + 2 * t * t * hd, 2 * d * hd + 14 * t * hd)
    return in_vmem(query_kernel, [], [x, w_query, keys, values], outs, [], price, "queries_scores")


def norm_kernel(slots, sv_ref, q_ref, kv_ref, og_ref, gain_ref, *rest):
    group = (len(rest) - 4) // 2
    prefixes, (datt_ref, term_ref, grad_ref), outs = rest[:group], rest[group : group + 3], rest[group + 3 : -1]
    state_ref = rest[-1]
    take_in(slots[0], prefixes, state_ref)
    t, hd = q_ref.shape
    for h in range(hd // DH):
        at = head(h)
        term = None
        state = state_ref[h]
        for p in range(PARTS):
            rows = part_rows(t, p)
            if p:
                state = state + kv_ref[p - 1, h]
            query = q_ref[rows, at]
            attended = sv_ref[rows, at] + mm(query, state.astype(BF16))
            inverse = lax.rsqrt(jnp.mean(attended * attended, axis=-1, keepdims=True) + 1e-06)
            normed = attended * inverse
            grad = og_ref[rows, at].astype(F32)
            more = jnp.sum(grad * normed, axis=0, keepdims=True)
            term = more if term is None else term + more
            d_normed = grad * gain_ref[:, at]
            inner = jnp.mean(d_normed * normed, axis=-1, keepdims=True)
            d_att = ((d_normed - normed * inner) * inverse).astype(BF16)
            datt_ref[rows, at] = d_att
            grad_ref[p, h] = mm_tn(query, d_att)
        term_ref[:, at] = term
    hand_out(slots[1], grad_ref, outs)


def norm_gradient(slots, sv, queries, prefixes, part_kv, out_grad, gain):
    t, hd = sv.shape
    heads = hd // DH
    group = len(prefixes)
    outs = [shape((t, hd), BF16), shape((1, hd), F32), shape((PARTS, heads, DH, DH), F32)]
    outs += [shape((heads // group, DH, DH), F32)] * group
    return in_vmem(
        norm_kernel, [slots], [sv, queries, part_kv, out_grad, gain, *prefixes], outs,
        [pltpu.VMEM((heads, DH, DH), F32)], cost(4 * t * hd * DH, 10 * t * hd), "norm_gradient",
    )


def store_wide(refs, rows, h, grad):
    width = refs[0].shape[1]
    start = h * DH % width
    refs[h * DH // width][rows, start : start + DH] = grad.astype(F32)


def dquery_kernel(slots, datt_ref, v_ref, k_ref, kv_ref, slope_ref, *rest):
    prefixes, (g16_ref, state_ref) = rest[:-2], rest[-2:]
    take_in(slots[0], prefixes, state_ref)
    t, hd = datt_ref.shape
    mask = causal_mask(t // PARTS, False)
    for h in range(hd // DH):
        at = head(h)
        state = state_ref[h]
        for p in range(PARTS):
            rows = part_rows(t, p)
            if p:
                state = state + kv_ref[p - 1, h]
            d_att = datt_ref[rows, at]
            back = masked(mask, mm_nt(d_att, v_ref[rows, at]))
            d_query = mm(back, k_ref[rows, at]) + mm_nt(d_att, state.astype(BF16))
            grad = (d_query * slope_ref[rows, at]).astype(BF16)
            g16_ref[rows, at] = grad


def query_gradient(slots, d_att, values, keys, prefixes, part_kv, slope):
    t, hd = d_att.shape
    return in_vmem(
        dquery_kernel, [slots], [d_att, values, keys, part_kv, slope, *prefixes],
        [shape((t, hd), BF16)], [pltpu.VMEM((hd // DH, DH, DH), F32)],
        cost(2 * t * t * hd, 16 * t * hd), "query_gradient",
    )[0]


def widen_kernel(grad_ref, *wide):
    width = wide[0].shape[1]
    for index, ref in enumerate(wide):
        ref[...] = grad_ref[:, index * width : (index + 1) * width].astype(F32)


def widen(grad):
    t, hd = grad.shape
    outs = [shape((t, hd // SHARES), F32)] * SHARES
    return in_vmem(widen_kernel, [], [grad], outs, [], cost(0, 0), "widen")


def within_kernel(datt_ref, v_ref, k_ref, q_ref, dk_ref, dv_ref):
    t, hd = datt_ref.shape
    mask = causal_mask(t // PARTS, True)
    for h in range(hd // DH):
        at = head(h)
        for p in range(PARTS):
            rows = part_rows(t, p)
            d_att, query = datt_ref[rows, at], q_ref[rows, at]
            back = masked(mask, mm_nt(v_ref[rows, at], d_att))
            dk_ref[rows, at] = mm(back, query)
            scores = masked(mask, mm_nt(k_ref[rows, at], query))
            dv_ref[rows, at] = mm(scores, d_att)


def within_block(d_att, values, keys, queries):
    t, hd = d_att.shape
    return in_vmem(
        within_kernel, [], [d_att, values, keys, queries], [shape((t, hd), F32)] * 2, [],
        cost(4 * t * t * hd, 16 * t * hd), "within_block",
    )


def dkv_kernel(slots, dk_ref, dv_ref, v_ref, k_ref, grad_ref, slope_ref, *rest):
    suffixes, outs, state_ref = rest[: -3 - 2 * SHARES], rest[-3 - 2 * SHARES : -1], rest[-1]
    (k16, *wide_k), (v16, *wide_v) = outs[: 1 + SHARES], outs[1 + SHARES :]
    take_in(slots[1], suffixes, state_ref)
    t, hd = dk_ref.shape
    for h in range(hd // DH):
        at = head(h)
        state = state_ref[h]
        for p in reversed(range(PARTS)):
            rows = part_rows(t, p)
            if p < PARTS - 1:
                state = state + grad_ref[p + 1, h]
            suffix = state.astype(BF16)
            d_key = dk_ref[rows, at] + mm_nt(v_ref[rows, at], suffix)
            grad = (d_key * slope_ref[rows, at]).astype(BF16)
            k16[rows, at] = grad
            store_wide(wide_k, rows, h, grad)
            grad = (dv_ref[rows, at] + mm(k_ref[rows, at], suffix)).astype(BF16)
            v16[rows, at] = grad
            store_wide(wide_v, rows, h, grad)


def key_value_gradients(slots, dk, dv, values, keys, suffixes, part_grad, slope):
    t, hd = dk.shape
    return in_vmem(
        dkv_kernel, [slots], [dk, dv, values, keys, part_grad, slope, *suffixes],
        ([shape((t, hd), BF16)] + [shape((t, hd // SHARES), F32)] * SHARES) * 2,
        [pltpu.VMEM((hd // DH, DH, DH), F32)],
        cost(4 * t * hd * DH, 28 * t * hd), "key_value_gradients",
    )


class Order:
    def __init__(self):
        self.last = None

    def tied(self, *arrays):
        if self.last is not None:
            *arrays, _ = lax.optimization_barrier((*arrays, self.last))
        return arrays[0] if len(arrays) == 1 else tuple(arrays)

    def mark(self, array):
        self.last = array


def exchange(array, axis, mask):
    count = lax.axis_size(axis)
    return lax.ppermute(array, axis, [(i, i ^ mask) for i in range(count)])


def combine_kernel(inner, base_ref, *refs):
    group = len(refs) // 2
    blocks, outs = refs[:group], refs[group:]
    for mask, out_ref in enumerate(outs):
        out_ref[...] = base_ref[...]
        for other, block in enumerate(blocks):
            if other != mask:

                @pl.when((inner[0] ^ other) < (inner[0] ^ mask))
                def _(out_ref=out_ref, block=block):
                    out_ref[...] += block[...]


def combine(inner, base, blocks):
    outs = [shape(base.shape, F32)] * len(blocks)
    return list(in_vmem(combine_kernel, [inner], [base, *blocks], outs, [], cost(0, 0), "combine"))


class Entering:
    def __init__(self, reverse):
        self.reverse = reverse
        self.count = lax.axis_size("seq")
        self.group = min(HEADS // PAIR, self.count)
        place = lax.axis_index("seq")
        if reverse:
            place = self.count - 1 - place
        self.inner, cluster = place % self.group, place // self.group
        self.twist = self.group // 2
        self.slot = (self.inner ^ (self.twist * (cluster % 2))).astype(jnp.int32)
        self.inner = self.inner.astype(jnp.int32)

    def first(self, pieces):
        self.blocks = [pieces[0]]
        for mask in range(1, self.group):
            self.blocks.append(exchange(pieces[mask], "seq", mask))

    def second(self, order):
        self.blocks[1:] = order.tied(*self.blocks[1:])
        total = sum(self.blocks[1:], self.blocks[0])
        order.mark(total)
        group, twist, count = self.group, self.twist, self.count
        clusters = count // group
        self.bases = []
        for shift in range(1, clusters):
            pairs = []
            for source in range(clusters - shift):
                for slot in range(group):
                    a = source * group + (slot ^ (twist * (source % 2)))
                    target = source + shift
                    b = target * group + (slot ^ (twist * (target % 2)))
                    pairs.append((count - 1 - a, count - 1 - b) if self.reverse else (a, b))
            self.bases.append(lax.ppermute(total, "seq", pairs))

    def third(self, order):
        bases = order.tied(*self.bases)
        if len(self.bases) == 1:
            bases = (bases,)
        base = sum(bases[1:], bases[0])
        self.outs = combine(self.inner, base, self.blocks)
        order.mark(self.outs[0])
        for mask in range(1, self.group):
            self.outs[mask] = exchange(self.outs[mask], "seq", mask)

    def result(self, order):
        self.outs[1:] = order.tied(*self.outs[1:])
        return self.outs


def both_exchange(array, masks):
    total = lax.axis_size("seq") * lax.axis_size("dp")
    return lax.ppermute(array, AXES, [(i, i ^ masks[i % 2]) for i in range(total)])


def turn_kernel(me_ref, x_ref, own_ref, other_ref, turned_ref):
    chips, rows, t = own_ref.shape
    core, chip = me_ref[0] % 2, me_ref[0] // 2
    span = 128 // (2 * rows)
    for block in range(chips // span):
        turned_ref[block] = jnp.transpose(x_ref[:, block * 128 : (block + 1) * 128])
    for block in range(chips // span):
        for i in range(span):
            slot = (block * span + i) ^ chip
            mine = pl.multiple_of((2 * i + core) * rows, rows)
            theirs = pl.multiple_of((2 * i + 1 - core) * rows, rows)
            own_ref[slot] = turned_ref[block, pl.ds(mine, rows)]
            other_ref[slot] = turned_ref[block, pl.ds(theirs, rows)].astype(F32)


def turn(me, x, chips):
    t, d = x.shape
    rows = d // (2 * chips)
    return in_vmem(
        turn_kernel, [me], [x], [shape((chips, rows, t), BF16), shape((chips, rows, t), F32)],
        [pltpu.VMEM((d // 128, 128, t), BF16)], cost(0, 12 * t * d), "turn_inputs",
    )


def merge_kernel(own_ref, other_ref, out_ref):
    half = own_ref.shape[-1]
    out_ref[:, :, :half] = own_ref[...]
    out_ref[:, :, half:] = other_ref[...].astype(BF16)


def merge(own, other):
    chips, rows, t = own.shape
    outs = [shape((chips, rows, 2 * t), BF16)]
    return in_vmem(merge_kernel, [], [own, other], outs, [], cost(0, 10 * own.size), "merge_inputs")[0]


def product_kernel(parts, me_ref, x_ref, own_ref, *rest):
    other_refs, out_refs = rest[: -len(parts)], rest[-len(parts) :]
    core = me_ref[0] % 2
    other = jnp.concatenate([ref[...].astype(BF16) for ref in other_refs], axis=1)
    for out_ref, (slots, start, stop) in zip(out_refs, parts):
        grads = jnp.concatenate([own_ref[:, start:stop], other[:, start:stop]], axis=0)
        rows = jnp.concatenate([x_ref[a ^ (core * (a ^ b))] for a, b in slots], axis=0)
        out_ref[...] = mm(rows, grads)


def products(me, x, own, others, parts, name):
    rows = x.shape[1]
    outs = [shape((len(slots) * rows, stop - start), F32) for slots, start, stop in parts]
    kernel = functools.partial(product_kernel, parts)
    return in_vmem(kernel, [me], [x, own, *others], outs, [], cost(0, 0), name)


def sent_kernel(slots, me_ref, x_ref, own_ref, *rest):
    other_refs, (out_hbm, out_ref, sems) = rest[:-3], rest[-3:]
    core = me_ref[0] % 2
    rows = jnp.concatenate([x_ref[a ^ (core * (a ^ b))] for a, b in slots], axis=0)
    share = other_refs[0].shape[1]
    copies = []
    for start in range(0, own_ref.shape[1], WIDE):
        other = other_refs[start // share][:, start % share : start % share + WIDE]
        grads = jnp.concatenate([own_ref[:, start : start + WIDE], other.astype(BF16)], axis=0)
        out_ref[:, start : start + WIDE] = mm(rows, grads)
        at = pl.ds(start, WIDE)
        copies.append(pltpu.make_async_copy(out_ref.at[:, at], out_hbm.at[:, at], sems.at[len(copies)]))
        copies[-1].start()
    for copy in copies:
        copy.wait()


def sent_products(me, x, own, others, slots, name):
    out = shape((len(slots) * x.shape[1], own.shape[1]), F32)
    size = sum(math.prod(a.shape) * a.dtype.itemsize for a in [x, own, *others, out])
    return pl.pallas_call(
        functools.partial(sent_kernel, slots),
        in_specs=[SMEM] + [VMEM] * (2 + len(others)),
        out_specs=HBM,
        out_shape=out,
        scratch_shapes=[pltpu.VMEM(out.shape, F32), pltpu.SemaphoreType.DMA((own.shape[1] // WIDE,))],
        compiler_params=params(size),
        cost_estimate=cost(0, 0),
        name=name,
    )(me, x, own, *others)


class Chunk:
    def __init__(self, start, stop, orders, masks):
        self.start, self.stop = start, stop
        self.orders = [[masks[axis] for axis in order] for order in orders]
        self.step = 0

    def slots(self, sent):
        out = []
        for masks in self.orders:
            mine = []
            for pick in range(1 << (len(masks) - 1)):
                slot = masks[0] >> 1 if sent else 0
                for place, mask in enumerate(masks[1:]):
                    if pick >> (len(masks) - 2 - place) & 1:
                        slot ^= mask >> 1
                mine.append(slot)
            out.append(mine)
        return tuple(zip(*out))

    def masks(self, step):
        return [masks[step] for masks in self.orders]

    def launch(self, sending):
        self.got = both_exchange(sending, self.masks(self.step))
        self.step += 1

    def advance(self, order, small=None):
        rest, got = self.rest, order.tied(self.got)
        extra = got.shape[0] - rest.shape[0]
        if self.step == len(self.orders[0]):
            self.rest = None
            if extra:
                self.out, small = add_last(rest, got, small)
                order.mark(small)
                return small
            self.out = rest + got
            order.mark(got)
            return None
        half = rest.shape[0] // 2
        if small is None:
            sending = add_rows(rest, got, half, half)
        else:
            sending, small = add_rows_with(rest, got, small)
        order.mark(sending)
        self.launch(sending)
        self.rest = add_rows(rest, order.tied(got), 0, half)
        order.mark(self.rest)
        return small


def add_kernel(start, a_ref, b_ref, out_ref):
    rows = slice(start, start + out_ref.shape[0])
    out_ref[...] = a_ref[rows] + b_ref[rows]


def add_rows(a, b, start, rows):
    outs = [shape((rows, a.shape[1]), F32)]
    kernel = functools.partial(add_kernel, start)
    return in_vmem(kernel, [], [a, b], outs, [], cost(0, 0), "add_rows")[0]


def add_with_kernel(rest_ref, got_ref, small_ref, sending_ref, sum_ref):
    full = rest_ref.shape[0]
    half = full // 2
    total = small_ref[...]
    if got_ref.shape[0] > full:
        total = total + got_ref[full:]
    sum_ref[...] = total
    sending_ref[half:] = total
    sending_ref[:half] = rest_ref[half:] + got_ref[half:full]


def add_rows_with(rest, got, small):
    outs = [shape((rows, rest.shape[1]), F32) for rows in (rest.shape[0] // 2 + small.shape[0], small.shape[0])]
    return in_vmem(add_with_kernel, [], [rest, got, small], outs, [], cost(0, 0), "add_rows_with")


def add_last_kernel(rest_ref, got_ref, small_ref, out_ref, sum_ref):
    full = rest_ref.shape[0]
    out_ref[...] = rest_ref[...] + got_ref[:full]
    sum_ref[...] = small_ref[...] + got_ref[full:]


def add_last(rest, got, small):
    outs = [shape(rest.shape, F32), shape(small.shape, F32)]
    return in_vmem(add_last_kernel, [], [rest, got, small], outs, [], cost(0, 0), "add_last")


def first_input_kernel(grad_ref, w_ref, out_ref):
    out_ref[...] = mm_nt(grad_ref[...], w_ref[...])


def rest_input_kernel(first_ref, codes_ref, grad_a, grad_b, wa_ref, wb_ref, out_ref, term_ref):
    total = first_ref[...] + mm_nt(grad_a[...], wa_ref[...]) + mm_nt(grad_b[...], wb_ref[...])
    out_ref[...] = total.astype(BF16)
    term_ref[...] = jnp.dot(
        codes_ref[...], total, precision=lax.Precision.HIGHEST, preferred_element_type=F32
    )


def row_blocks(w):
    return pl.BlockSpec((WIDE, w.shape[1]), lambda i: (i, 0))


def out_columns(rows):
    return pl.BlockSpec((rows, WIDE), lambda i: (0, i))


def first_input_gradient(grad, w):
    t, d = grad.shape[0], w.shape[0]
    return pl.pallas_call(
        first_input_kernel,
        grid=(d // WIDE,),
        in_specs=[VMEM, row_blocks(w)],
        out_specs=out_columns(t),
        out_shape=shape((t, d), F32),
        compiler_params=params(4 * t * WIDE * 4 + 2 * grad.size),
        cost_estimate=cost(0, 0),
        name="input_gradient_q",
    )(grad, w)


def rest_input_gradient(first, codes, grad_a, grad_b, wa, wb):
    t, d = first.shape
    rows = codes.shape[0]
    size = 4 * t * WIDE * 4 + 4 * grad_a.size
    return pl.pallas_call(
        rest_input_kernel,
        grid=(d // WIDE,),
        in_specs=[out_columns(t), VMEM, VMEM, VMEM, row_blocks(wa), row_blocks(wb)],
        out_specs=[out_columns(t), out_columns(rows)],
        out_shape=[shape((t, d), BF16), shape((rows, d), F32)],
        compiler_params=params(size),
        cost_estimate=cost(0, 0),
        name="input_gradient_kv",
    )(first, codes, grad_a, grad_b, wa, wb)


def body(resid, token_ids, code_proj, w_query, w_key, w_value, gain, out_grad):
    positions, width = resid.shape[1:]
    features = w_query.shape[1]
    n_dp = lax.axis_size("dp")
    total = lax.axis_size("seq") * n_dp
    me = (lax.axis_index("seq") * n_dp + lax.axis_index("dp")).astype(jnp.int32).reshape(1)
    order = Order()

    before, after = Entering(False), Entering(True)
    slots = jnp.stack([before.slot, after.slot])
    before.inner, after.inner = before.inner.reshape(1), after.inner.reshape(1)
    slots, me, before.inner, after.inner = lax.optimization_barrier((slots, me, before.inner, after.inner))
    x, code_values, keys, key_slope, values, part_kv, *pieces = embed_keys_values(
        slots, resid[0], token_ids, code_proj, w_key, w_value, before.group
    )
    before.first(pieces)
    queries, query_slope, within = queries_scores(x, w_query, keys, values)
    order.mark(within)
    own_rows, other_rows = turn(me, order.tied(x), total // 2)
    order.mark(own_rows)
    before.second(order)
    other_rows = both_exchange(order.tied(other_rows), (1, 1))
    before.third(order)
    prefixes = before.result(order)

    d_att, gain_term, part_grad, *pieces = norm_gradient(
        slots, within, queries, prefixes, part_kv, out_grad[0], gain.reshape(1, features)
    )
    order.mark(d_att)
    after.first(pieces)
    grad_q = query_gradient(slots, order.tied(d_att), values, keys, prefixes, part_kv, query_slope)
    order.mark(grad_q)
    merged = merge(own_rows, order.tied(other_rows))
    order.mark(merged)
    after.second(order)
    wide_q = widen(order.tied(grad_q))
    order.mark(wide_q[0])
    wide_q = [both_exchange(share, (1, 1)) for share in wide_q]
    dk, dv = within_block(order.tied(d_att), values, keys, queries)
    order.mark(dk)

    bits = total.bit_length() - 1
    masks = [1 << b for b in range(1, bits)]
    masks[-1] |= masks[-2]
    dims = len(masks)

    unit = features // 8
    extra = tuple(range(4, dims))

    def chunks_of(plan):
        out, start = [], 0
        for units, *orders in plan:
            axes = [tuple("xyzw".index(name) for name in order) + extra for order in orders]
            out.append(Chunk(start * unit, (start + units) * unit, axes, masks))
            start += units
        return out

    chunks_q = chunks_of([(8, "xzwy", "zxyw")])
    chunks_k = chunks_of([(8, "xzwy", "yxzw")])
    chunks_v = chunks_of([(8, "zyxw", "yxzw")])
    every = chunks_q + chunks_k + chunks_v

    def begin(chunks, own, others, name):
        own, *others = order.tied(own, *others)
        sent = [sent_products(me, merged, own, others, c.slots(True), name) for c in chunks]
        order.mark(sent[0])
        for chunk, array in zip(chunks, sent):
            chunk.launch(array)
        kept = products(me, merged, order.tied(own), others, [(c.slots(False), c.start, c.stop) for c in chunks], name + "_kept")
        order.mark(kept[0])
        for chunk, array in zip(chunks, kept):
            chunk.rest = array

    begin(chunks_q, grad_q, wide_q, "weight_q")
    after.third(order)
    input_grad = first_input_gradient(order.tied(grad_q), w_query)
    order.mark(input_grad)
    suffixes = after.result(order)
    outs = key_value_gradients(slots, dk, dv, values, keys, suffixes, part_grad, key_slope)
    (grad_k, *wide_k), (grad_v, *wide_v) = outs[: 1 + SHARES], outs[1 + SHARES :]
    order.mark(grad_k)
    wide_k = [both_exchange(share, (1, 1)) for share in wide_k]
    wide_v = [both_exchange(share, (1, 1)) for share in wide_v]
    begin(chunks_k, grad_k, wide_k, "weight_k")
    begin(chunks_v, grad_v, wide_v, "weight_v")
    resid_grad, code_term = rest_input_gradient(
        input_grad, code_values, order.tied(grad_k), grad_v, w_key, w_value
    )
    order.mark(code_term)
    grad_scale = 1.0 / math.sqrt(positions * total)
    codes = len(fsq_levels)
    carrier = chunks_q[0]
    edge = carrier.stop - carrier.start
    small = jnp.concatenate([gain_term.reshape(-1), code_term[:codes].reshape(-1)])
    used = small.shape[0]
    small = jnp.pad(small, (0, -used % (8 * edge))).reshape(-1, edge)

    def advance(index):
        nonlocal small
        if every[index] is carrier:
            small = carrier.advance(order, small)
        else:
            every[index].advance(order)

    small = small + order.tied(both_exchange(small, (1, 1)))
    order.mark(small)
    for index in (0, 1, 0, 2, 1, 0, 2, 1, 2):
        advance(index)
    while any(c.step < dims for c in every):
        for index in (0, 1, 2):
            if every[index].step < dims:
                advance(index)
    advance(0)
    small = small + order.tied(both_exchange(small, carrier.masks(0)))
    order.mark(small)
    for index in (1, 2):
        advance(index)
    small = small.reshape(-1)[:used] * grad_scale
    gain_sum, code_sum = small[:features], small[features:].reshape(codes, width)

    def joined(chunks):
        return jnp.concatenate([c.out for c in chunks], axis=-1)

    weights = jnp.stack([joined(chunks_q), joined(chunks_k), joined(chunks_v)], axis=1) * grad_scale
    return resid_grad[None], weights, gain_sum, code_sum


def solution(mesh):
    return jax.shard_map(
        body,
        mesh=mesh,
        in_specs=(
            P("dp", "seq", None),
            P("dp", "seq"),
            P(),
            P(),
            P(),
            P(),
            P(),
            P("dp", "seq", None),
        ),
        out_specs=(P("dp", "seq", None), P(AXES, None, None), P(), P()),
        check_vma=False,
    )
```
